32 devices in a mesh: groups: 2 (over x), wide: 16 (over z, y, core).
Axes of the slice: x: 2, y: 2, z: 4, core: 2. Of those that a mesh axis runs over, the one named last changes fastest.
Arguments:
- pair: bfloat16 [512, 256, 128], P(('groups', 'wide')), parts along dimension 0, may hold values from -6 to 6
- residue_mask: int32 [512], P('groups'), parts along dimension 0, may hold values from 0 to 1, as said below
- input_gain: float32 [128], replicated, may hold values from 0.25 to 1.75
- left_gate: bfloat16 [128, 128], replicated, may hold values from -0.5 to 0.5
- left_value: bfloat16 [128, 128], replicated, may hold values from -0.5 to 0.5
- right_gate: bfloat16 [128, 128], replicated, may hold values from -0.5 to 0.5
- right_value: bfloat16 [128, 128], replicated, may hold values from -0.5 to 0.5
- middle_gain: float32 [128], replicated, may hold values from 0.25 to 1.75
- output_gate: bfloat16 [128, 128], replicated, may hold values from -0.5 to 0.5
- output_value: bfloat16 [128, 128], replicated, may hold values from -0.5 to 0.5
Outputs:
- pair_next: bfloat16 [512, 256, 128], P('groups', 'wide'), parts along dimension 0
The draws below stay inside these ranges and needn't reach their ends.
There are 2 independent parts, one for each index of `groups`. The reference program is written for one: setup_inputs(seed, part) draws one part's arguments, and reference() takes and returns one part's arrays. A program takes and returns all parts, laid end to end along the dimension named above; an argument that names none is the same for every part. Nothing has to cross between parts.
Inputs may be any that keep to these rules, and one draw needn't show every extreme that they name: `residue_mask`: 1 on a leading run of residues of length 128 or more and 0 after it; the last residue is always 0.
All inputs are finite; a program needn't handle non-finite values.
Results may differ from the reference program's by a relative error of at most 0.0035.
Values may be sent and summed in bfloat16 or wider, within the bound.
No kernel may reach another device: no remote copies, remote signals or barrier semaphores. Data moves between devices by JAX's collectives and lax.ppermute only.
A program may use at most 64 MiB of HBM per device.

```python
import jax
import jax.numpy as jnp
from jax import lax

CHANNELS = 128
HIDDEN_SIZE = 128
RESIDUES = 256


def draw_residue_mask(key, part):
    key = jax.random.fold_in(key, 7)
    length = RESIDUES // 2 + jax.random.randint(key, (), 0, RESIDUES // 2)
    return (jnp.arange(RESIDUES) < length).astype(jnp.int32)


def shard_levels(stream_key, extent, cuts, low, high):
    factor_of = 1.0
    for axis_at, blocks in cuts:
        steps = jax.random.uniform(jax.random.fold_in(jax.random.fold_in(stream_key, 6), axis_at), (blocks,), jnp.float32, low / len(cuts), high / len(cuts))
        factor_of = factor_of * jnp.repeat(jnp.exp(steps), extent[axis_at] // blocks).reshape((-1,) + (1,) * (len(extent) - 1 - axis_at))
    return factor_of


def bell_draw(key, shape, width, reach, pieces=(), dtype=jnp.bfloat16):
    array = jax.random.normal(key, shape, jnp.float32) * width
    if len(pieces) > 0:
        array = shard_levels(key, shape, pieces, -0.22, 0.18) * array
    return jnp.clip(array, min=-reach, max=reach).astype(dtype)


def setup_inputs(seed: int = 0, part: int = 0) -> dict:
    streams_of = jax.random.split(jax.random.key(seed), 11)
    part_splits = jax.random.split(jax.random.fold_in(streams_of[10], part), 11)
    return {
        "pair": bell_draw(part_splits[0], (RESIDUES, RESIDUES, CHANNELS), 1.0, 6.0, ((0, 16),)),
        "residue_mask": draw_residue_mask(jax.random.fold_in(jax.random.fold_in(streams_of[10], part), 71), part),
        "input_gain": jnp.clip(1.0 + 0.15 * jax.random.normal(streams_of[2], (CHANNELS,), jnp.float32), 0.25, 1.75),
        "left_gate": bell_draw(streams_of[3], (CHANNELS, HIDDEN_SIZE), CHANNELS ** -0.5, 0.5),
        "left_value": bell_draw(streams_of[4], (CHANNELS, HIDDEN_SIZE), CHANNELS ** -0.5, 0.5),
        "right_gate": bell_draw(streams_of[5], (CHANNELS, HIDDEN_SIZE), CHANNELS ** -0.5, 0.5),
        "right_value": bell_draw(streams_of[6], (CHANNELS, HIDDEN_SIZE), CHANNELS ** -0.5, 0.5),
        "middle_gain": jnp.clip(1.0 + 0.15 * jax.random.normal(streams_of[7], (HIDDEN_SIZE,), jnp.float32), 0.25, 1.75),
        "output_gate": bell_draw(streams_of[8], (CHANNELS, CHANNELS), CHANNELS ** -0.5, 0.5),
        "output_value": bell_draw(streams_of[9], (HIDDEN_SIZE, CHANNELS), HIDDEN_SIZE ** -0.5, 0.5),
    }


def layer_norm(values, gain, axis):
    mean_value = lax.optimization_barrier(jnp.mean(values, axis=axis, keepdims=True))
    centred = values - mean_value
    variance = lax.optimization_barrier(jnp.mean(centred * centred, axis=axis, keepdims=True))
    return centred * lax.rsqrt(variance + 1e-05) * gain

def edge_side(flat_normed, gate_weight, value_weight, pair_mask):
    gated = jnp.dot(flat_normed, gate_weight, preferred_element_type=jnp.float32)
    valued = jnp.dot(flat_normed, value_weight, preferred_element_type=jnp.float32)
    count = pair_mask.shape[0]
    edges = (jax.nn.sigmoid(gated) * valued).reshape(count, count, -1) * pair_mask[:, :, None]
    return jnp.transpose(edges.astype(jnp.bfloat16), (2, 0, 1))

def reference(pair, residue_mask, input_gain, left_gate, left_value, right_gate, right_value, middle_gain, output_gate, output_value):
    count = pair.shape[0]
    channels = pair.shape[2]
    pair_float = pair.astype(jnp.float32)
    normed = layer_norm(pair_float, input_gain, 2).astype(jnp.bfloat16)
    flat_normed = normed.reshape(count * count, channels)
    chain_mask = residue_mask.astype(jnp.float32)
    pair_mask = chain_mask[:, None] * chain_mask[None, :]
    left_edges = edge_side(flat_normed, left_gate, left_value, pair_mask)
    right_edges = edge_side(flat_normed, right_gate, right_value, pair_mask)

    def one_channel(operands):
        return jnp.dot(operands[0], operands[1].T, preferred_element_type=jnp.float32).astype(jnp.bfloat16)
    triangle = lax.map(one_channel, (left_edges, right_edges))
    middle = layer_norm(triangle.astype(jnp.float32), middle_gain[:, None, None], 0).astype(jnp.bfloat16)
    hidden_count = middle.shape[0]
    projected = jnp.dot(middle.reshape(hidden_count, count * count).T, output_value, preferred_element_type=jnp.float32)
    gating = jax.nn.sigmoid(jnp.dot(flat_normed, output_gate, preferred_element_type=jnp.float32))
    update = (gating * projected).reshape(count, count, channels)
    return (pair_float + update).astype(jnp.bfloat16)
```

```python
import jax
import jax.numpy as jnp
from jax import lax
from jax.sharding import PartitionSpec as P


def layer_norm(values, gain, axis):
    mean_value = jnp.mean(values, axis=axis, keepdims=True)
    centred = values - mean_value
    variance = jnp.mean(centred * centred, axis=axis, keepdims=True)
    return centred * lax.rsqrt(variance + 1e-05) * gain


def swap(values, mask, count):
    return lax.ppermute(values, "wide", [(d, d ^ mask) for d in range(count)])


def edge_side(normed, gate_weight, value_weight, pair_mask):
    gated = jnp.einsum("ikc,ch->hik", normed, gate_weight, preferred_element_type=jnp.float32)
    valued = jnp.einsum("ikc,ch->hik", normed, value_weight, preferred_element_type=jnp.float32)
    return (jax.nn.sigmoid(gated) * valued * pair_mask[None, :, :]).astype(jnp.bfloat16)


def gather(own, bits, count):
    units = {0: own}
    for bit in bits:
        for mask in list(units):
            units[mask | bit] = swap(units[mask], bit, count)
    return units


def make_shards(count):
    bits = [1 << b for b in range(count.bit_length() - 1)]
    right_bits = bits[0::2][::-1]
    left_bits = bits[1::2][::-1]

    def shards(
        pair,
        residue_mask,
        input_gain,
        left_gate,
        left_value,
        right_gate,
        right_value,
        middle_gain,
        output_gate,
        output_value,
    ):
        rows = pair.shape[0]
        me = lax.axis_index("wide")
        chain_mask = residue_mask.astype(jnp.float32)

        def mask_of(unit):
            own_mask = lax.dynamic_slice_in_dim(chain_mask, (me ^ unit) * rows, rows, 0)
            return own_mask[:, None] * chain_mask[None, :]

        def norm(values):
            return layer_norm(values.astype(jnp.float32), input_gain, 2).astype(jnp.bfloat16)

        left_rows = gather(pair, left_bits, count)
        own_normed = norm(pair)
        right_own = edge_side(own_normed, right_gate, right_value, mask_of(0))
        right_units = gather(right_own, right_bits, count)
        right_order = list(right_units)
        right_edges = jnp.concatenate([right_units[m] for m in right_order], axis=1)

        result = {}
        for unit, raw in left_rows.items():
            normed = own_normed if unit == 0 else norm(raw)
            left = edge_side(normed, left_gate, left_value, mask_of(unit))
            triangle = jnp.einsum(
                "hik,hjk->hij", left, right_edges, preferred_element_type=jnp.float32
            ).astype(jnp.bfloat16)
            middle = layer_norm(
                triangle.astype(jnp.float32), middle_gain[:, None, None], 0
            ).astype(jnp.bfloat16)
            projected = jnp.einsum(
                "hij,hc->ijc", middle, output_value, preferred_element_type=jnp.float32
            )
            columns = lambda v: jnp.concatenate(
                [lax.dynamic_slice_in_dim(v, (me ^ m) * rows, rows, 1) for m in right_order], axis=1
            )
            gating = jax.nn.sigmoid(
                jnp.einsum("ijc,cd->ijd", columns(normed), output_gate, preferred_element_type=jnp.float32)
            )
            out = (columns(raw).astype(jnp.float32) + gating * projected).astype(jnp.bfloat16)
            for at, m in enumerate(right_order):
                block = out[:, at * rows : (at + 1) * rows]
                result[unit | m] = block if m == 0 else swap(block, m, count)
        stacked = jnp.stack([result[m] for m in range(count)])
        picked = stacked[me ^ jnp.arange(count)]
        return picked.reshape(count * rows, rows, pair.shape[2])

    return shards


def solution(mesh):
    in_specs = (P(("groups", "wide"), None, None), P("groups")) + (P(),) * 8
    out_specs = P("groups", "wide", None)
    return jax.shard_map(
        make_shards(mesh.shape["wide"]), mesh=mesh, in_specs=in_specs, out_specs=out_specs, check_vma=False
    )
```

```python
import functools

import jax
import jax.numpy as jnp
from jax import lax
from jax.experimental import pallas as pl
from jax.experimental.pallas import tpu as pltpu
from jax.sharding import PartitionSpec as P

LANES = 128
WIDE_TYPE = jnp.float32
NARROW = jnp.bfloat16
LAST_BY_LAST = (((1,), (1,)), ((), ()))
VMEM = pl.BlockSpec(memory_space=pltpu.VMEM)
SMEM = pl.BlockSpec(memory_space=pltpu.SMEM)
ANY = pl.BlockSpec(memory_space=pl.ANY)


SHORT = pl.CostEstimate(flops=1 << 20, bytes_accessed=1 << 10, transcendentals=0)
LONG = pl.CostEstimate(flops=1 << 35, bytes_accessed=1 << 10, transcendentals=0)


def sigmoid(values):
    return 0.5 * jnp.tanh(0.5 * values) + 0.5


def norm_rows(values, gain):
    values = values.astype(WIDE_TYPE)
    mean_value = jnp.mean(values, axis=1, keepdims=True)
    centred = values - mean_value
    variance = jnp.mean(centred * centred, axis=1, keepdims=True)
    return (centred * lax.rsqrt(variance + 1e-05) * gain).astype(NARROW)


def fill_edges(first, at, total, pair_ref, chain_ref, mask_ref, gain_ref, weight_refs, edges):
    rows, _, channels = pair_ref.shape
    hidden = weight_refs[0].shape[1]
    gain = jnp.broadcast_to(gain_ref[...], (channels, channels)).T[:, :1]
    weights = jnp.concatenate([ref[...].T for ref in weight_refs], axis=0)
    column_mask = mask_ref[...].astype(WIDE_TYPE)

    def one_row(i, carry):
        values = pair_ref[i].astype(WIDE_TYPE).T
        mean_value = jnp.mean(values, axis=0, keepdims=True)
        centred = values - mean_value
        variance = jnp.mean(centred * centred, axis=0, keepdims=True)
        normed = (centred * lax.rsqrt(variance + 1e-05) * gain).astype(NARROW)
        both = jnp.dot(weights, normed, preferred_element_type=WIDE_TYPE)
        row_mask = chain_ref[first + i].astype(WIDE_TYPE)
        masked = sigmoid(both[:hidden]) * both[hidden:] * (column_mask * row_mask)
        for part in range(len(edges)):
            edges[part][pl.ds(at + i, hidden, stride=total), :] = masked[
                :, part * LANES : (part + 1) * LANES
            ]
        return carry

    lax.fori_loop(0, rows, one_row, 0, unroll=8)


def read_edges(edges, start, size):
    return jnp.concatenate([part[pl.ds(start, size), :] for part in edges], axis=1).astype(NARROW)


def edge_kernel(unit, me_ref, chain_ref, pair_ref, mask_ref, gain_ref, gate_ref, value_ref, out_ref, *edges):
    rows = pair_ref.shape[0]
    first = (me_ref[0] ^ unit) * rows
    fill_edges(first, 0, rows, pair_ref, chain_ref, mask_ref, gain_ref, (gate_ref, value_ref), edges)

    def one_channel(h, carry):
        out_ref[h] = read_edges(edges, pl.multiple_of(h * rows, rows), rows)
        return carry

    lax.fori_loop(0, out_ref.shape[0], one_channel, 0, unroll=16)


def left_kernel(unit, offset, me_ref, chain_ref, pair_ref, mask_ref, gain_ref, gate_ref, value_ref, *edges):
    rows = pair_ref.shape[0]
    first = (me_ref[0] ^ unit) * offset[1] + offset[0]
    fill_edges(first, 0, rows, pair_ref, chain_ref, mask_ref, gain_ref, (gate_ref, value_ref), edges)


def triangle_kernel(
    count, order, me_ref, middle_gain_ref, gain_ref, output_gate_ref, output_value_ref, *rest
):
    units = len(order)
    right_refs, rest = rest[:units], rest[units:]
    pair_refs, rest = rest[:count], rest[count:]
    out_refs, triangle = rest[-1 - units : -1], rest[-1]
    parts = pair_refs[0].shape[1] // LANES
    left_refs = [rest[n * parts : (n + 1) * parts] for n in range(count)]
    me = me_ref[0]
    sizes = [ref.shape[0] for ref in pair_refs]
    rows = sum(sizes)
    hidden = output_value_ref.shape[0]
    width = right_refs[0].shape[1]
    span = units * width
    starts = [sum(sizes[:n]) for n in range(count)]

    def read_left(h):
        whole = [
            jnp.concatenate([ref[pl.ds(pl.multiple_of(h * size, size), size), :] for ref in refs], axis=1)
            for refs, size in zip(left_refs, sizes)
        ]
        return jnp.concatenate(whole, axis=0).astype(NARROW)

    def multiply(h, total):
        at = pl.multiple_of(h * rows, rows)
        left = read_left(h)
        right = jnp.concatenate([ref[h] for ref in right_refs], axis=0)
        product = lax.dot_general(left, right, LAST_BY_LAST, preferred_element_type=WIDE_TYPE)
        product = product.astype(NARROW).astype(WIDE_TYPE)
        triangle[pl.ds(at, rows), :span] = product
        return total + product

    zeros = jnp.zeros((rows, span), WIDE_TYPE)
    mean_value = lax.fori_loop(0, hidden, multiply, zeros, unroll=16) * (1.0 / hidden)

    def spread(h, total):
        centred = triangle[pl.ds(pl.multiple_of(h * rows, rows), rows), :span] - mean_value
        return total + centred * centred

    variance = lax.fori_loop(0, hidden, spread, zeros, unroll=16) * (1.0 / hidden)
    scale = lax.rsqrt(variance + 1e-05)

    def normalise(h, carry):
        at = pl.multiple_of(h * rows, rows)
        triangle[pl.ds(at, rows), :span] = (
            (triangle[pl.ds(at, rows), :span] - mean_value) * scale * middle_gain_ref[h]
        )
        return carry

    lax.fori_loop(0, hidden, normalise, 0, unroll=16)
    for n in range(count):

        def finish(i, carry):
            row = starts[n] + i
            middle = triangle[pl.ds(row, hidden, stride=rows), :].T[:span].astype(NARROW)
            projected = jnp.dot(middle, output_value_ref[...], preferred_element_type=WIDE_TYPE)
            base = jnp.concatenate(
                [
                    pair_refs[n][i, pl.ds(pl.multiple_of((me ^ unit) * width, width), width), :]
                    for unit in order
                ],
                axis=0,
            )
            normed = norm_rows(base, gain_ref[...])
            gating = sigmoid(jnp.dot(normed, output_gate_ref[...], preferred_element_type=WIDE_TYPE))
            updated = (base.astype(WIDE_TYPE) + gating * projected).astype(NARROW)
            for u in range(units):
                out_refs[u][row] = updated[u * width : (u + 1) * width]
            return carry

        lax.fori_loop(0, sizes[n], finish, 0, unroll=4)


def place_kernel(places, me_ref, *rest):
    count = len(places)
    in_refs, out_ref, sem = rest[:count], rest[count], rest[count + 1]
    me = me_ref[0]
    copies = []
    for n, place in enumerate(places):
        for unit, start, size, offset, width in place:
            copies.append(
                pltpu.make_async_copy(
                    in_refs[n].at[pl.ds(start, size)],
                    out_ref.at[pl.ds((me ^ unit) * width + offset, size)],
                    sem.at[len(copies)],
                )
            )
    for copy in copies:
        copy.start()
    for copy in copies:
        copy.wait()


def edge_scratch(rows, hidden, residues):
    return [pltpu.VMEM((hidden * rows, LANES), WIDE_TYPE)] * (residues // LANES)


def edge_call(unit, me, chain, pair, mask, gain, gate, value):
    rows, residues, _ = pair.shape
    hidden = gate.shape[1]
    return pl.pallas_call(
        functools.partial(edge_kernel, unit),
        out_shape=jax.ShapeDtypeStruct((hidden, rows, residues), NARROW),
        in_specs=[SMEM] * 2 + [VMEM] * 5,
        out_specs=VMEM,
        scratch_shapes=edge_scratch(rows, hidden, residues),
        compiler_params=pltpu.CompilerParams(vmem_limit_bytes=16 << 20),
        cost_estimate=pl.CostEstimate(flops=1 << 20, bytes_accessed=1 << 10, transcendentals=0),
        name="edges",
    )(me, chain, pair, mask, gain, gate, value)


def left_call(unit, offset, cost, me, chain, pair, mask, gain, gate, value):
    rows, residues, _ = pair.shape
    hidden = gate.shape[1]
    return pl.pallas_call(
        functools.partial(left_kernel, unit, offset),
        out_shape=[jax.ShapeDtypeStruct((hidden * rows, LANES), WIDE_TYPE)] * (residues // LANES),
        in_specs=[SMEM] * 2 + [VMEM] * 5,
        out_specs=[VMEM] * (residues // LANES),
        compiler_params=pltpu.CompilerParams(vmem_limit_bytes=16 << 20),
        cost_estimate=cost,
        name="left_edges",
    )(me, chain, pair, mask, gain, gate, value)


def triangle_call(order, me, middle_gain, gain, output_gate, output_value, right, pairs, lefts):
    _, _, channels = pairs[0].shape
    rows = sum(p.shape[0] for p in pairs)
    hidden = output_value.shape[0]
    width = right[0].shape[1]
    tensors = [gain, output_gate, output_value, *right, *pairs]
    for left in lefts:
        tensors += left
    return pl.pallas_call(
        functools.partial(triangle_kernel, len(pairs), order),
        out_shape=[jax.ShapeDtypeStruct((rows, width, channels), NARROW)] * len(order),
        in_specs=[SMEM] * 2 + [VMEM] * len(tensors),
        out_specs=[VMEM] * len(order),
        scratch_shapes=[pltpu.VMEM((hidden * rows, LANES), WIDE_TYPE)],
        compiler_params=pltpu.CompilerParams(vmem_limit_bytes=40 << 20),
        cost_estimate=pl.CostEstimate(flops=1 << 20, bytes_accessed=1 << 10, transcendentals=0),
        name="triangle",
    )(me, middle_gain, *tensors)


def place_call(places, me, blocks, shape):
    return pl.pallas_call(
        functools.partial(place_kernel, places),
        out_shape=jax.ShapeDtypeStruct(shape, NARROW),
        in_specs=[SMEM] + [ANY] * len(blocks),
        out_specs=ANY,
        scratch_shapes=[pltpu.SemaphoreType.DMA((sum(len(p) for p in places),))],
        compiler_params=pltpu.CompilerParams(vmem_limit_bytes=8 << 20),
        name="place",
    )(me, *blocks)


def make_shards(count):
    bits = [1 << b for b in range(count.bit_length() - 1)]
    right_bits = bits[0::2][::-1]
    left_bits = bits[1::2][::-1]
    pieces = 2

    def swap(values, mask):
        return lax.ppermute(values, "wide", [(d, d ^ mask) for d in range(count)])

    def shards(
        pair,
        residue_mask,
        input_gain,
        left_gate,
        left_value,
        right_gate,
        right_value,
        middle_gain,
        output_gate,
        output_value,
    ):
        rows = pair.shape[0]
        me = lax.axis_index("wide").astype(jnp.int32).reshape(1)
        mask = residue_mask.reshape(1, -1)
        gain = input_gain.reshape(1, -1)
        part = rows // pieces
        far_bit, near_bits = left_bits[0], left_bits[1:]

        far = [swap(pair[n * part : (n + 1) * part], far_bit) for n in range(pieces)]
        near = {0: pair}
        for bit in near_bits:
            for unit in list(near):
                near[unit | bit] = swap(near[unit], bit)
        own_right = edge_call(0, me, residue_mask, pair, mask, gain, right_gate, right_value)
        right = {0: own_right}
        for bit in right_bits:
            for unit in list(right):
                right[unit | bit] = swap(right[unit], bit)
        order = list(right)
        rights = [right[unit] for unit in order]

        far_units = {far_bit: far}
        for bit in near_bits:
            for unit in list(far_units):
                far_units[unit | bit] = [swap(piece, bit) for piece in far_units[unit]]

        blocks = []
        places = []

        def left_edges(unit, offset, raw, cost):
            return left_call(
                unit, (offset, rows), cost, me, residue_mask, raw, mask, gain, left_gate, left_value
            )

        def finish(firsts, pairs, lefts):
            outs = triangle_call(
                order, me, middle_gain, gain, output_gate, output_value, rights, pairs, lefts
            )
            for unit, out in zip(order, outs):
                blocks.append(out if unit == 0 else swap(out, unit))
                place, start = [], 0
                for (left_unit, offset), source in zip(firsts, pairs):
                    place.append((left_unit | unit, start, source.shape[0], offset, rows))
                    start += source.shape[0]
                places.append(place)

        lefts = []
        after = own_right
        for unit, raw in near.items():
            raw, after = lax.optimization_barrier((raw, after))
            lefts.append(left_edges(unit, 0, raw, SHORT))
            after = lefts[-1][0]
        finish([(unit, 0) for unit in near], list(near.values()), lefts)
        for unit, raws in far_units.items():
            lefts = [left_edges(unit, n * part, raws[n], LONG) for n in range(pieces)]
            finish([(unit, n * part) for n in range(pieces)], raws, lefts)
        return place_call(places, me, blocks, (count * rows, rows, pair.shape[2]))

    return shards


def solution(mesh):
    in_specs = (P(("groups", "wide"), None, None), P("groups")) + (P(),) * 8
    out_specs = P("groups", "wide", None)
    return jax.shard_map(
        make_shards(mesh.shape["wide"]), mesh=mesh, in_specs=in_specs, out_specs=out_specs, check_vma=False
    )
```

```python
import functools

import jax
import jax.numpy as jnp
from jax import lax
from jax.experimental import pallas as pl
from jax.experimental.pallas import tpu as pltpu
from jax.sharding import PartitionSpec as P

LANES = 128
WIDE_TYPE = jnp.float32
NARROW = jnp.bfloat16
LAST_BY_LAST = (((1,), (1,)), ((), ()))
VMEM = pl.BlockSpec(memory_space=pltpu.VMEM)
SMEM = pl.BlockSpec(memory_space=pltpu.SMEM)
ANY = pl.BlockSpec(memory_space=pl.ANY)


SHORT = pl.CostEstimate(flops=1 << 20, bytes_accessed=1 << 10, transcendentals=0)
LONG = pl.CostEstimate(flops=1 << 35, bytes_accessed=1 << 10, transcendentals=0)


def sigmoid(values):
    return 0.5 * jnp.tanh(0.5 * values) + 0.5


def norm_rows(values, gain):
    values = values.astype(WIDE_TYPE)
    mean_value = jnp.mean(values, axis=1, keepdims=True)
    centred = values - mean_value
    variance = jnp.mean(centred * centred, axis=1, keepdims=True)
    return (centred * lax.rsqrt(variance + 1e-05) * gain).astype(NARROW)


def fill_edges(first, at, total, pair_ref, chain_ref, mask_ref, gain_ref, weight_refs, edges):
    rows, _, channels = pair_ref.shape
    hidden = weight_refs[0].shape[1]
    gain = jnp.broadcast_to(gain_ref[...], (channels, channels)).T[:, :1]
    weights = jnp.concatenate([ref[...].T for ref in weight_refs], axis=0)
    column_mask = mask_ref[...].astype(WIDE_TYPE)

    def one_row(i, carry):
        values = pair_ref[i].astype(WIDE_TYPE).T
        mean_value = jnp.mean(values, axis=0, keepdims=True)
        centred = values - mean_value
        variance = jnp.mean(centred * centred, axis=0, keepdims=True)
        normed = (centred * lax.rsqrt(variance + 1e-05) * gain).astype(NARROW)
        both = jnp.dot(weights, normed, preferred_element_type=WIDE_TYPE)
        row_mask = chain_ref[first + i].astype(WIDE_TYPE)
        masked = sigmoid(both[:hidden]) * both[hidden:] * (column_mask * row_mask)
        for part in range(len(edges)):
            edges[part][pl.ds(at + i, hidden, stride=total), :] = masked[
                :, part * LANES : (part + 1) * LANES
            ]
        return carry

    lax.fori_loop(0, rows, one_row, 0, unroll=min(rows, 8))


def read_edges(edges, start, size):
    return jnp.concatenate([part[pl.ds(start, size), :] for part in edges], axis=1).astype(NARROW)


def edge_kernel(unit, me_ref, chain_ref, pair_ref, mask_ref, gain_ref, gate_ref, value_ref, out_ref, *edges):
    rows = pair_ref.shape[0]
    first = (me_ref[0] ^ unit) * rows
    fill_edges(first, 0, rows, pair_ref, chain_ref, mask_ref, gain_ref, (gate_ref, value_ref), edges)

    def one_channel(h, carry):
        out_ref[h] = read_edges(edges, pl.multiple_of(h * rows, rows), rows)
        return carry

    lax.fori_loop(0, out_ref.shape[0], one_channel, 0, unroll=16)


def left_kernel(unit, span, offsets, keep, me_ref, chain_ref, mask_ref, gain_ref, gate_ref, value_ref, *rest):
    count = len(offsets)
    pair_refs, edges = rest[:count], rest[count:]
    if keep:
        edges, copy_ref = edges[:-1], edges[-1]
        copy_ref[...] = pair_refs[0][...]
    total = sum(ref.shape[0] for ref in pair_refs)
    at = 0
    for offset, pair_ref in zip(offsets, pair_refs):
        first = (me_ref[0] ^ unit) * span + offset
        fill_edges(first, at, total, pair_ref, chain_ref, mask_ref, gain_ref, (gate_ref, value_ref), edges)
        at += pair_ref.shape[0]


def triangle_kernel(
    count, order, me_ref, middle_gain_ref, gain_ref, output_gate_ref, output_value_ref, *rest
):
    units = len(order)
    right_refs, rest = rest[:units], rest[units:]
    pair_refs, rest = rest[:count], rest[count:]
    out_refs, triangle = rest[-1 - units : -1], rest[-1]
    parts = pair_refs[0].shape[1] // LANES
    left_refs = [rest[n * parts : (n + 1) * parts] for n in range((len(rest) - 1 - units) // parts)]
    left_sizes = [refs[0].shape[0] // output_value_ref.shape[0] for refs in left_refs]
    me = me_ref[0]
    sizes = [ref.shape[0] for ref in pair_refs]
    rows = sum(sizes)
    hidden = output_value_ref.shape[0]
    width = right_refs[0].shape[1]
    span = units * width
    starts = [sum(sizes[:n]) for n in range(count)]

    def read_left(h):
        whole = [
            jnp.concatenate([ref[pl.ds(pl.multiple_of(h * size, size), size), :] for ref in refs], axis=1)
            for refs, size in zip(left_refs, left_sizes)
        ]
        return jnp.concatenate(whole, axis=0).astype(NARROW)

    def multiply(h, total):
        at = pl.multiple_of(h * rows, rows)
        left = read_left(h)
        right = jnp.concatenate([ref[h] for ref in right_refs], axis=0)
        product = lax.dot_general(left, right, LAST_BY_LAST, preferred_element_type=WIDE_TYPE)
        product = product.astype(NARROW).astype(WIDE_TYPE)
        triangle[pl.ds(at, rows), :span] = product
        return total + product

    zeros = jnp.zeros((rows, span), WIDE_TYPE)
    mean_value = lax.fori_loop(0, hidden, multiply, zeros, unroll=16) * (1.0 / hidden)

    def spread(h, total):
        centred = triangle[pl.ds(pl.multiple_of(h * rows, rows), rows), :span] - mean_value
        return total + centred * centred

    variance = lax.fori_loop(0, hidden, spread, zeros, unroll=16) * (1.0 / hidden)
    scale = lax.rsqrt(variance + 1e-05)

    def normalise(h, carry):
        at = pl.multiple_of(h * rows, rows)
        triangle[pl.ds(at, rows), :span] = (
            (triangle[pl.ds(at, rows), :span] - mean_value) * scale * middle_gain_ref[h]
        )
        return carry

    lax.fori_loop(0, hidden, normalise, 0, unroll=16)
    for n in range(count):

        def finish(i, carry):
            row = starts[n] + i
            middle = triangle[pl.ds(row, hidden, stride=rows), :].T[:span].astype(NARROW)
            projected = jnp.dot(middle, output_value_ref[...], preferred_element_type=WIDE_TYPE)
            base = jnp.concatenate(
                [
                    pair_refs[n][i, pl.ds(pl.multiple_of((me ^ unit) * width, width), width), :]
                    for unit in order
                ],
                axis=0,
            )
            normed = norm_rows(base, gain_ref[...])
            gating = sigmoid(jnp.dot(normed, output_gate_ref[...], preferred_element_type=WIDE_TYPE))
            updated = (base.astype(WIDE_TYPE) + gating * projected).astype(NARROW)
            for u in range(units):
                out_refs[u][row] = updated[u * width : (u + 1) * width]
            return carry

        lax.fori_loop(0, sizes[n], finish, 0, unroll=min(sizes[n], 4))


def place_kernel(places, me_ref, *rest):
    count = len(places)
    in_refs, out_ref, sem = rest[:count], rest[count], rest[count + 1]
    me = me_ref[0]
    copies = []
    for n, place in enumerate(places):
        for unit, start, size, offset, width in place:
            copies.append(
                pltpu.make_async_copy(
                    in_refs[n].at[pl.ds(start, size)],
                    out_ref.at[pl.ds((me ^ unit) * width + offset, size)],
                    sem.at[len(copies)],
                )
            )
    for copy in copies:
        copy.start()
    for copy in copies:
        copy.wait()


def behind(kernel, count):
    def body(*refs):
        kernel(*refs[count:])

    return body


def edge_scratch(rows, hidden, residues):
    return [pltpu.VMEM((hidden * rows, LANES), WIDE_TYPE)] * (residues // LANES)


def edge_call(deps, unit, me, chain, pair, mask, gain, gate, value):
    rows, residues, _ = pair.shape
    hidden = gate.shape[1]
    return pl.pallas_call(
        behind(functools.partial(edge_kernel, unit), len(deps)),
        out_shape=jax.ShapeDtypeStruct((hidden, rows, residues), NARROW),
        in_specs=[ANY] * len(deps) + [SMEM] * 2 + [VMEM] * 5,
        out_specs=VMEM,
        scratch_shapes=edge_scratch(rows, hidden, residues),
        compiler_params=pltpu.CompilerParams(vmem_limit_bytes=16 << 20),
        cost_estimate=pl.CostEstimate(flops=1 << 20, bytes_accessed=1 << 10, transcendentals=0),
        name="edges",
    )(*deps, me, chain, pair, mask, gain, gate, value)


def left_call(deps, unit, span, offsets, keep, cost, me, chain, mask, gain, gate, value, pairs):
    rows = sum(p.shape[0] for p in pairs)
    residues = pairs[0].shape[1]
    hidden = gate.shape[1]
    shapes = [jax.ShapeDtypeStruct((hidden * rows, LANES), WIDE_TYPE)] * (residues // LANES)
    if keep:
        shapes.append(jax.ShapeDtypeStruct(pairs[0].shape, NARROW))
    return pl.pallas_call(
        behind(functools.partial(left_kernel, unit, span, offsets, keep), len(deps)),
        out_shape=shapes,
        in_specs=[ANY] * len(deps) + [SMEM] * 2 + [VMEM] * (4 + len(pairs)),
        out_specs=[VMEM] * len(shapes),
        compiler_params=pltpu.CompilerParams(vmem_limit_bytes=16 << 20),
        cost_estimate=cost,
        name="left_edges",
    )(*deps, me, chain, mask, gain, gate, value, *pairs)


def triangle_call(deps, order, me, middle_gain, gain, output_gate, output_value, right, pairs, lefts):
    _, _, channels = pairs[0].shape
    rows = sum(p.shape[0] for p in pairs)
    hidden = output_value.shape[0]
    width = right[0].shape[1]
    tensors = [gain, output_gate, output_value, *right, *pairs]
    for left in lefts:
        tensors += left
    return pl.pallas_call(
        behind(functools.partial(triangle_kernel, len(pairs), order), len(deps)),
        out_shape=[jax.ShapeDtypeStruct((rows, width, channels), NARROW)] * len(order),
        in_specs=[ANY] * len(deps) + [SMEM] * 2 + [VMEM] * len(tensors),
        out_specs=[VMEM] * len(order),
        scratch_shapes=[pltpu.VMEM((hidden * rows, LANES), WIDE_TYPE)],
        compiler_params=pltpu.CompilerParams(vmem_limit_bytes=40 << 20),
        cost_estimate=pl.CostEstimate(flops=1 << 20, bytes_accessed=1 << 10, transcendentals=0),
        name="triangle",
    )(*deps, me, middle_gain, *tensors)


def place_call(places, me, blocks, shape):
    return pl.pallas_call(
        functools.partial(place_kernel, places),
        out_shape=jax.ShapeDtypeStruct(shape, NARROW),
        in_specs=[SMEM] + [ANY] * len(blocks),
        out_specs=ANY,
        scratch_shapes=[pltpu.SemaphoreType.DMA((sum(len(p) for p in places),))],
        compiler_params=pltpu.CompilerParams(vmem_limit_bytes=8 << 20),
        name="place",
    )(me, *blocks)


def hold_kernel(*refs):
    pass


def hold(value, *deps):
    return pl.pallas_call(
        hold_kernel,
        out_shape=jax.ShapeDtypeStruct(value.shape, value.dtype),
        in_specs=[ANY] * (1 + len(deps)),
        out_specs=ANY,
        input_output_aliases={0: 0},
        compiler_params=pltpu.CompilerParams(vmem_limit_bytes=1 << 20),
        cost_estimate=SHORT,
        name="hold",
    )(value, *deps)


def make_shards(count):
    bits = [1 << b for b in range(count.bit_length() - 1)]
    right_bits = bits[0::2][::-1]
    left_bits = bits[1::2][::-1]

    def swap(values, mask):
        return lax.ppermute(values, "wide", [(d, d ^ mask) for d in range(count)])

    def shards(
        pair,
        residue_mask,
        input_gain,
        left_gate,
        left_value,
        right_gate,
        right_value,
        middle_gain,
        output_gate,
        output_value,
    ):
        rows = pair.shape[0]
        me = lax.axis_index("wide").astype(jnp.int32).reshape(1)
        mask = residue_mask.reshape(1, -1)
        gain = input_gain.reshape(1, -1)
        far_bit, near_bits = left_bits[0], left_bits[1:]
        cuts = [(0, rows // 2), (rows // 2, rows // 2)]

        def gather(own, bits):
            units = {0: own}
            for bit in bits:
                for unit in list(units):
                    units[unit | bit] = swap(units[unit], bit)
            return units

        def left_edges(deps, unit, pieces, cost, raws, keep=False):
            offsets = tuple(start for start, _ in pieces)
            return left_call(
                deps, unit, rows, offsets, keep, cost, me, residue_mask, mask, gain, left_gate, left_value, raws
            )

        blocks = []
        places = []

        def finish(deps, sources, pairs, lefts):
            outs = triangle_call(
                deps, order, me, middle_gain, gain, output_gate, output_value, rights, pairs, lefts
            )
            for unit, out in zip(order, outs):
                blocks.append(out if unit == 0 else swap(out, unit))
                place, start = [], 0
                for (left_unit, offset), source in zip(sources, pairs):
                    place.append((left_unit | unit, start, source.shape[0], offset, rows))
                    start += source.shape[0]
                places.append(place)
            return outs[0]

        whole = ((0, rows),)
        far = [swap(pair[start : start + size], far_bit) for start, size in cuts]
        near = gather(pair, near_bits)
        own_right = edge_call((), 0, me, residue_mask, pair, mask, gain, right_gate, right_value)
        lefts = []
        for unit, raw in near.items():
            cost = LONG if unit else SHORT
            lefts.append(left_edges(() if unit else (own_right,), unit, whole, cost, [raw]))
        far_first = left_edges((), far_bit, cuts[:1], LONG, far[:1])

        right = {0: own_right}
        for bit in right_bits:
            for unit in list(right):
                moved = swap(right[unit], bit)
                if bit == right_bits[0]:
                    moved = hold(moved, far_first[0], lefts[0][0])
                right[unit | bit] = moved
        order = list(right)
        rights = [right[unit] for unit in order]

        far_last = left_edges((), far_bit, cuts[1:], SHORT, far[1:])
        done = finish(
            (),
            [(unit, 0) for unit in near] + [(far_bit, start) for start, _ in cuts],
            list(near.values()) + far,
            lefts + [far_first, far_last],
        )
        pieces = [gather(piece, near_bits) for piece in far]
        for unit in list(near)[1:]:
            raws = [piece[unit] for piece in pieces]
            edges = left_edges((done,), far_bit | unit, cuts, SHORT, raws)
            finish((), [(far_bit | unit, start) for start, _ in cuts], raws, [edges])
        return place_call(places, me, blocks, (count * rows, rows, pair.shape[2]))

    return shards


def solution(mesh):
    in_specs = (P(("groups", "wide"), None, None), P("groups")) + (P(),) * 8
    out_specs = P("groups", "wide", None)
    return jax.shard_map(
        make_shards(mesh.shape["wide"]), mesh=mesh, in_specs=in_specs, out_specs=out_specs, check_vma=False
    )
```

```python
import functools

import jax
import jax.numpy as jnp
from jax import lax
from jax.experimental import pallas as pl
from jax.experimental.pallas import tpu as pltpu
from jax.sharding import PartitionSpec as P

LANES = 128
WIDE_TYPE = jnp.float32
NARROW = jnp.bfloat16
LAST_BY_LAST = (((1,), (1,)), ((), ()))
VMEM = pl.BlockSpec(memory_space=pltpu.VMEM)
SMEM = pl.BlockSpec(memory_space=pltpu.SMEM)
ANY = pl.BlockSpec(memory_space=pl.ANY)


SHORT = pl.CostEstimate(flops=1 << 20, bytes_accessed=1 << 10, transcendentals=0)
LONG = pl.CostEstimate(flops=1 << 35, bytes_accessed=1 << 10, transcendentals=0)


def sigmoid(values):
    return 0.5 * jnp.tanh(0.5 * values) + 0.5


def norm_rows(values, gain):
    values = values.astype(WIDE_TYPE)
    mean_value = jnp.mean(values, axis=1, keepdims=True)
    centred = values - mean_value
    variance = jnp.mean(centred * centred, axis=1, keepdims=True)
    return (centred * lax.rsqrt(variance + 1e-05) * gain).astype(NARROW)


def home_of(me, unit, base):
    far_bit, low_bit = base
    inner = jnp.where((me & far_bit) != 0, 1, 0) ^ jnp.where((me & low_bit) != 0, 1, 0)
    return me ^ unit ^ (inner * (far_bit | low_bit))


def fill_edges(first, at, rows, total, load, chain_ref, mask_ref, gain_ref, weight_refs, edges):
    channels, hidden = weight_refs[0].shape
    gain = jnp.broadcast_to(gain_ref[...], (channels, channels)).T[:, :1]
    weights = jnp.concatenate([ref[...].T for ref in weight_refs], axis=0)
    column_mask = mask_ref[...].astype(WIDE_TYPE)

    def one_row(i, carry):
        values = load(i).T
        mean_value = jnp.mean(values, axis=0, keepdims=True)
        centred = values - mean_value
        variance = jnp.mean(centred * centred, axis=0, keepdims=True)
        normed = (centred * lax.rsqrt(variance + 1e-05) * gain).astype(NARROW)
        both = jnp.dot(weights, normed, preferred_element_type=WIDE_TYPE)
        row_mask = chain_ref[first + i].astype(WIDE_TYPE)
        masked = sigmoid(both[:hidden]) * both[hidden:] * (column_mask * row_mask)
        for part in range(len(edges)):
            edges[part][pl.ds(at + i, hidden, stride=total), :] = masked[
                :, part * LANES : (part + 1) * LANES
            ]
        return carry

    lax.fori_loop(0, rows, one_row, 0, unroll=min(rows, 8))


def read_edges(edges, start, size):
    return jnp.concatenate([part[pl.ds(start, size), :] for part in edges], axis=1).astype(NARROW)


def edge_kernel(unit, count, me_ref, chain_ref, mask_ref, gain_ref, gate_ref, value_ref, *rest):
    pair_refs, out_ref, edges = rest[:count], rest[count], rest[count + 1 :]
    rows = out_ref.shape[1]
    at = 0
    for pair_ref in pair_refs:
        size = pair_ref.shape[0]
        first = (me_ref[0] ^ unit) * rows + at
        load = lambda i: pair_ref[i].astype(WIDE_TYPE)
        fill_edges(first, at, size, rows, load, chain_ref, mask_ref, gain_ref, (gate_ref, value_ref), edges)
        at += size

    def one_channel(h, carry):
        out_ref[h] = read_edges(edges, pl.multiple_of(h * rows, rows), rows)
        return carry

    lax.fori_loop(0, out_ref.shape[0], one_channel, 0, unroll=16)


def left_kernel(unit, base, span, offsets, me_ref, chain_ref, mask_ref, gain_ref, gate_ref, value_ref, *rest):
    count = len(offsets)
    pair_refs, edges = rest[:count], rest[count:]
    total = sum(ref.shape[0] for ref in pair_refs)
    at = 0
    for offset, pair_ref in zip(offsets, pair_refs):
        size = pair_ref.shape[0]
        first = home_of(me_ref[0], unit, base) * span + offset
        load = lambda i: pair_ref[i].astype(WIDE_TYPE)
        fill_edges(first, at, size, total, load, chain_ref, mask_ref, gain_ref, (gate_ref, value_ref), edges)
        at += size


def triangle_kernel(
    count, order, me_ref, middle_gain_ref, gain_ref, output_gate_ref, output_value_ref, *rest
):
    units = len(order)
    right_refs, rest = rest[:units], rest[units:]
    pair_refs, rest = rest[:count], rest[count:]
    out_refs, triangle = rest[-1 - units : -1], rest[-1]
    parts = pair_refs[0].shape[1] // LANES
    left_refs = [rest[n * parts : (n + 1) * parts] for n in range((len(rest) - 1 - units) // parts)]
    left_sizes = [refs[0].shape[0] // output_value_ref.shape[0] for refs in left_refs]
    me = me_ref[0]
    sizes = [ref.shape[0] for ref in pair_refs]
    rows = sum(sizes)
    hidden = output_value_ref.shape[0]
    width = right_refs[0].shape[1]
    span = units * width

    def read_left(h):
        whole = [
            jnp.concatenate([ref[pl.ds(pl.multiple_of(h * size, size), size), :] for ref in refs], axis=1)
            for refs, size in zip(left_refs, left_sizes)
        ]
        return jnp.concatenate(whole, axis=0).astype(NARROW)

    fold = 2 if rows >= 32 and rows % 16 == 0 and 2 * span <= LANES else 1
    deep = rows // fold
    lower = lax.broadcasted_iota(jnp.int32, (deep, fold * span), 1) < span

    def multiply(h, total):
        right = jnp.concatenate([ref[h] for ref in right_refs] * fold, axis=0)
        product = lax.dot_general(read_left(h), right, LAST_BY_LAST, preferred_element_type=WIDE_TYPE)
        if fold == 2:
            product = jnp.where(lower, product[:deep], product[deep:])
        product = product.astype(NARROW).astype(WIDE_TYPE)
        triangle[pl.ds(pl.multiple_of(h * deep, deep), deep), : fold * span] = product
        return total + product

    zeros = jnp.zeros((deep, fold * span), WIDE_TYPE)
    mean_value = lax.fori_loop(0, hidden, multiply, zeros, unroll=16) * (1.0 / hidden)

    def spread(h, total):
        at = pl.multiple_of(h * deep, deep)
        centred = triangle[pl.ds(at, deep), : fold * span] - mean_value
        return total + centred * centred

    variance = lax.fori_loop(0, hidden, spread, zeros, unroll=16) * (1.0 / hidden)
    scale = lax.rsqrt(variance + 1e-05)

    def normalise(h, carry):
        at = pl.multiple_of(h * deep, deep)
        triangle[pl.ds(at, deep), : fold * span] = (
            (triangle[pl.ds(at, deep), : fold * span] - mean_value) * scale * middle_gain_ref[h]
        )
        return carry

    lax.fori_loop(0, hidden, normalise, 0, unroll=16)
    homes = [(ref, i) for ref in pair_refs for i in range(ref.shape[0])]
    columns = [pl.multiple_of((me ^ unit) * width, width) for unit in order]
    for row in range(deep):
        middle = triangle[pl.ds(row, hidden, stride=deep), :].T[: fold * span].astype(NARROW)
        projected = jnp.dot(middle, output_value_ref[...], preferred_element_type=WIDE_TYPE)
        base = jnp.concatenate(
            [
                homes[row + f * deep][0][homes[row + f * deep][1], pl.ds(column, width), :]
                for f in range(fold)
                for column in columns
            ],
            axis=0,
        )
        normed = norm_rows(base, gain_ref[...])
        gating = sigmoid(jnp.dot(normed, output_gate_ref[...], preferred_element_type=WIDE_TYPE))
        updated = (base.astype(WIDE_TYPE) + gating * projected).astype(NARROW)
        for f in range(fold):
            for u in range(units):
                at = (f * units + u) * width
                out_refs[u][row + f * deep] = updated[at : at + width]


def place_kernel(places, base, rows, me_ref, *rest):
    count = len(places)
    in_refs, out_ref, sem = rest[:count], rest[count], rest[count + 1]
    me = me_ref[0]
    copies = []
    for n, (right_unit, parts) in enumerate(places):
        start = 0
        for unit, offset, size in parts:
            at = home_of(me ^ right_unit, unit, base) * rows + offset
            copies.append(
                pltpu.make_async_copy(
                    in_refs[n].at[pl.ds(start, size)], out_ref.at[pl.ds(at, size)], sem.at[len(copies)]
                )
            )
            start += size
    for copy in copies:
        copy.start()
    for copy in copies:
        copy.wait()


def behind(kernel, count):
    def body(*refs):
        kernel(*refs[count:])

    return body


def edge_scratch(rows, hidden, residues):
    return [pltpu.VMEM((hidden * rows, LANES), WIDE_TYPE)] * (residues // LANES)


def edge_call(deps, unit, me, chain, mask, gain, gate, value, pairs):
    rows = sum(p.shape[0] for p in pairs)
    residues = pairs[0].shape[1]
    hidden = gate.shape[1]
    return pl.pallas_call(
        behind(functools.partial(edge_kernel, unit, len(pairs)), len(deps)),
        out_shape=jax.ShapeDtypeStruct((hidden, rows, residues), NARROW),
        in_specs=[ANY] * len(deps) + [SMEM] * 2 + [VMEM] * (4 + len(pairs)),
        out_specs=VMEM,
        scratch_shapes=edge_scratch(rows, hidden, residues),
        compiler_params=pltpu.CompilerParams(vmem_limit_bytes=16 << 20),
        cost_estimate=SHORT,
        name="edges",
    )(*deps, me, chain, mask, gain, gate, value, *pairs)


def left_call(deps, unit, base, span, offsets, cost, me, chain, mask, gain, gate, value, pairs):
    rows = sum(p.shape[0] for p in pairs)
    residues = pairs[0].shape[1]
    hidden = gate.shape[1]
    shapes = [jax.ShapeDtypeStruct((hidden * rows, LANES), WIDE_TYPE)] * (residues // LANES)
    return pl.pallas_call(
        behind(functools.partial(left_kernel, unit, base, span, offsets), len(deps)),
        out_shape=shapes,
        in_specs=[ANY] * len(deps) + [SMEM] * 2 + [VMEM] * (4 + len(pairs)),
        out_specs=[VMEM] * len(shapes),
        compiler_params=pltpu.CompilerParams(vmem_limit_bytes=16 << 20),
        cost_estimate=cost,
        name="left_edges",
    )(*deps, me, chain, mask, gain, gate, value, *pairs)


def triangle_call(deps, order, me, middle_gain, gain, output_gate, output_value, right, pairs, lefts):
    _, _, channels = pairs[0].shape
    rows = sum(p.shape[0] for p in pairs)
    hidden = output_value.shape[0]
    width = right[0].shape[1]
    tensors = [gain, output_gate, output_value, *right, *pairs]
    for left in lefts:
        tensors += left
    return pl.pallas_call(
        behind(functools.partial(triangle_kernel, len(pairs), order), len(deps)),
        out_shape=[jax.ShapeDtypeStruct((rows, width, channels), NARROW)] * len(order),
        in_specs=[ANY] * len(deps) + [SMEM] * 2 + [VMEM] * len(tensors),
        out_specs=[VMEM] * len(order),
        scratch_shapes=[pltpu.VMEM((hidden * rows, LANES), WIDE_TYPE)],
        compiler_params=pltpu.CompilerParams(vmem_limit_bytes=40 << 20),
        cost_estimate=pl.CostEstimate(flops=1 << 20, bytes_accessed=1 << 10, transcendentals=0),
        name="triangle",
    )(*deps, me, middle_gain, *tensors)


def place_call(places, base, rows, me, blocks, shape):
    return pl.pallas_call(
        functools.partial(place_kernel, places, base, rows),
        out_shape=jax.ShapeDtypeStruct(shape, NARROW),
        in_specs=[SMEM] + [ANY] * len(blocks),
        out_specs=ANY,
        scratch_shapes=[pltpu.SemaphoreType.DMA((sum(len(parts) for _, parts in places),))],
        compiler_params=pltpu.CompilerParams(vmem_limit_bytes=8 << 20),
        name="place",
    )(me, *blocks)


def hold_kernel(*refs):
    pass


def hold(value, *deps, cost=SHORT):
    return pl.pallas_call(
        hold_kernel,
        out_shape=jax.ShapeDtypeStruct(value.shape, value.dtype),
        in_specs=[ANY] * (1 + len(deps)),
        out_specs=ANY,
        input_output_aliases={0: 0},
        compiler_params=pltpu.CompilerParams(vmem_limit_bytes=1 << 20),
        cost_estimate=cost,
        name="hold",
    )(value, *deps)


def split_kernel(count, in_ref, *rest):
    out_refs, sem = rest[:count], rest[count]
    size = in_ref.shape[0] // count
    copies = [
        pltpu.make_async_copy(in_ref.at[pl.ds(n * size, size)], out_refs[n], sem.at[n]) for n in range(count)
    ]
    for copy in copies:
        copy.start()
    for copy in copies:
        copy.wait()


def split_call(values, count):
    shape = (values.shape[0] // count, *values.shape[1:])
    return pl.pallas_call(
        functools.partial(split_kernel, count),
        out_shape=[jax.ShapeDtypeStruct(shape, values.dtype)] * count,
        in_specs=[ANY],
        out_specs=[VMEM] * count,
        scratch_shapes=[pltpu.SemaphoreType.DMA((count,))],
        compiler_params=pltpu.CompilerParams(vmem_limit_bytes=8 << 20),
        cost_estimate=SHORT,
        name="split",
    )(values)


def make_shards(count):
    bits = [1 << b for b in range(count.bit_length() - 1)]
    right_bits = bits[0::2][::-1]
    left_bits = bits[1::2][::-1]

    far_bit, near_bits = left_bits[0], left_bits[1:]
    low_bit = right_bits[0]
    base = (far_bit, low_bit)

    def swap(values, mask):
        return lax.ppermute(values, "wide", [(d, d ^ mask) for d in range(count)])

    def cross(values):
        inner = lambda d: bool(d & far_bit) != bool(d & low_bit)
        pairs = [(d, d ^ far_bit ^ low_bit if inner(d) else d) for d in range(count)]
        return lax.ppermute(values, "wide", pairs)

    def gather(own, bits):
        units = {0: own}
        for bit in bits:
            for unit in list(units):
                units[unit ^ bit] = swap(units[unit], bit)
        return units

    def shards(
        pair,
        residue_mask,
        input_gain,
        left_gate,
        left_value,
        right_gate,
        right_value,
        middle_gain,
        output_gate,
        output_value,
    ):
        rows = pair.shape[0]
        me = lax.axis_index("wide").astype(jnp.int32).reshape(1)
        mask = residue_mask.reshape(1, -1)
        gain = input_gain.reshape(1, -1)
        half = rows // 2
        offsets = (0, half)
        own = split_call(pair, 2)

        def right_edges(deps, unit, raws):
            return edge_call(deps, unit, me, residue_mask, mask, gain, right_gate, right_value, raws)

        def left_edges(deps, unit, at, cost, raws):
            return left_call(
                deps, unit, base, rows, at, cost, me, residue_mask, mask, gain, left_gate, left_value, raws
            )

        blocks = []
        places = []

        def finish(deps, sources, lefts):
            pairs = [raw for _, _, raw in sources]
            outs = triangle_call(
                deps, order, me, middle_gain, gain, output_gate, output_value, rights, pairs, lefts
            )
            parts = [(unit, offset, raw.shape[0]) for unit, offset, raw in sources]
            for unit, out in zip(order, outs):
                blocks.append(out if unit == 0 else swap(out, unit))
                places.append((unit, parts))
            return outs[0]

        side = [swap(piece, low_bit) for piece in own]
        first = [cross(piece) for piece in own]
        near_first = [gather(piece, near_bits) for piece in first]
        units = list(near_first[0])[1:]
        right_own = right_edges((), 0, own)
        right_side = right_edges((right_own, *[near_first[0][unit] for unit in units]), low_bit, side)
        right = {}
        for unit, edges in ((0, right_own), (low_bit, right_side)):
            for more, moved in gather(edges, right_bits[1:]).items():
                right[unit ^ more] = moved
        order = list(right)
        rights = [right[unit] for unit in order]
        second = [cross(piece) for piece in side]

        left_first = left_edges((right_side,), 0, offsets, SHORT, first)
        start = [(0, at, raw) for at, raw in zip(offsets, first)]
        early = [(unit, 0, near_first[0][unit]) for unit in units]
        lefts = [left_edges((left_first[0],), unit, (at,), SHORT, [raw]) for unit, at, raw in early]
        second[0] = hold(second[0], *[left[0] for left in lefts])
        late = [(low_bit, 0, second[0])] + [(unit, half, near_first[1][unit]) for unit in units]
        for unit, at, raw in late:
            lefts.append(left_edges((), unit, (at,), SHORT, [raw]))
        early[0] = (*early[0][:2], hold(early[0][2], lefts[len(early)][0], cost=LONG))
        done = finish((), start + early + late, [left_first] + lefts)
        sent = len(blocks)

        second[1] = hold(second[1], done)
        near_second = [gather(piece, near_bits) for piece in second]
        batch = [(low_bit, half, second[1])]
        batch += [(low_bit ^ unit, 0, near_second[0][unit]) for unit in units]
        lefts = [left_edges((done,), unit, (at,), SHORT, [raw]) for unit, at, raw in batch]
        done = finish((), batch, lefts)

        batch = [(low_bit ^ unit, half, near_second[1][unit]) for unit in units]
        deps = (done, *blocks[1:sent])
        lefts = [left_edges(deps, unit, (at,), SHORT, [raw]) for unit, at, raw in batch]
        finish((), batch, lefts)
        return place_call(places, base, rows, me, blocks, (count * rows, rows, pair.shape[2]))

    return shards


def solution(mesh):
    in_specs = (P(("groups", "wide"), None, None), P("groups")) + (P(),) * 8
    out_specs = P("groups", "wide", None)
    return jax.shard_map(
        make_shards(mesh.shape["wide"]), mesh=mesh, in_specs=in_specs, out_specs=out_specs, check_vma=False
    )
```

```python
import functools

import jax
import jax.numpy as jnp
from jax import lax
from jax.experimental import pallas as pl
from jax.experimental.pallas import tpu as pltpu
from jax.sharding import PartitionSpec as P

LANES = 128
WIDE_TYPE = jnp.float32
NARROW = jnp.bfloat16
LAST_BY_LAST = (((1,), (1,)), ((), ()))
VMEM = pl.BlockSpec(memory_space=pltpu.VMEM)
SMEM = pl.BlockSpec(memory_space=pltpu.SMEM)
ANY = pl.BlockSpec(memory_space=pl.ANY)


SHORT = pl.CostEstimate(flops=1 << 20, bytes_accessed=1 << 10, transcendentals=0)
LONG = pl.CostEstimate(flops=1 << 35, bytes_accessed=1 << 10, transcendentals=0)


def sigmoid(values):
    return 0.5 * jnp.tanh(0.5 * values) + 0.5


def norm_rows(values, gain):
    values = values.astype(WIDE_TYPE)
    mean_value = jnp.mean(values, axis=1, keepdims=True)
    centred = values - mean_value
    variance = jnp.mean(centred * centred, axis=1, keepdims=True)
    return (centred * lax.rsqrt(variance + 1e-05) * gain).astype(NARROW)


def home_of(me, unit, base):
    far_bit, low_bit = base
    inner = jnp.where((me & far_bit) != 0, 1, 0) ^ jnp.where((me & low_bit) != 0, 1, 0)
    return me ^ unit ^ (inner * (far_bit | low_bit))


def fill_edges(first, at, rows, total, load, chain_ref, mask_ref, gain_ref, weight_refs, edges):
    channels, hidden = weight_refs[0].shape
    gain = jnp.broadcast_to(gain_ref[...], (channels, channels)).T[:, :1]
    weights = jnp.concatenate([ref[...].T for ref in weight_refs], axis=0)
    column_mask = mask_ref[...].astype(WIDE_TYPE)

    def one_row(i, carry):
        values = load(i).T.astype(WIDE_TYPE)
        mean_value = jnp.mean(values, axis=0, keepdims=True)
        centred = values - mean_value
        variance = jnp.mean(centred * centred, axis=0, keepdims=True)
        normed = (centred * lax.rsqrt(variance + 1e-05) * gain).astype(NARROW)
        both = jnp.dot(weights, normed, preferred_element_type=WIDE_TYPE)
        row_mask = chain_ref[first + i].astype(WIDE_TYPE)
        masked = sigmoid(both[:hidden]) * both[hidden:] * (column_mask * row_mask)
        for part in range(len(edges)):
            edges[part][pl.ds(at + i, hidden, stride=total), :] = masked[
                :, part * LANES : (part + 1) * LANES
            ]
        return carry

    lax.fori_loop(0, rows, one_row, 0, unroll=min(rows, 8))


def read_rows(parts, h, size):
    at = pl.ds(pl.multiple_of(h * size, size), size)
    return jnp.concatenate([part[at, :] for part in parts], axis=1)


def edge_kernel(unit, offset, count, ready, me_ref, chain_ref, mask_ref, gain_ref, gate_ref, value_ref, *rest):
    pair_refs, ready_refs, out_ref, edges = rest[:count], rest[count:][:ready], rest[count + ready], rest[count + ready + 1 :]
    rows = out_ref.shape[1]
    fresh = sum(ref.shape[0] for ref in pair_refs)
    at = 0
    for pair_ref in pair_refs:
        size = pair_ref.shape[0]
        first = (me_ref[0] ^ unit) * rows + offset + at
        load = lambda i: pair_ref[i]
        fill_edges(first, at, size, fresh, load, chain_ref, mask_ref, gain_ref, (gate_ref, value_ref), edges)
        at += size

    def one_channel(h, carry):
        pieces = [(offset, read_rows(edges, h, fresh))]
        if ready:
            pieces.append((fresh - offset, read_rows(ready_refs, h, rows - fresh)))
        pieces.sort(key=lambda piece: piece[0])
        out_ref[h] = jnp.concatenate([piece for _, piece in pieces], axis=0).astype(NARROW)
        return carry

    lax.fori_loop(0, out_ref.shape[0], one_channel, 0, unroll=16)


def left_kernel(unit, base, span, offsets, me_ref, chain_ref, mask_ref, gain_ref, gate_ref, value_ref, *rest):
    count = len(offsets)
    pair_refs, edges = rest[:count], rest[count:]
    total = sum(ref.shape[0] for ref in pair_refs)
    at = 0
    for offset, pair_ref in zip(offsets, pair_refs):
        size = pair_ref.shape[0]
        home = me_ref[0] ^ unit if base is None else home_of(me_ref[0], unit, base)
        first = home * span + offset
        load = lambda i: pair_ref[i]
        fill_edges(first, at, size, total, load, chain_ref, mask_ref, gain_ref, (gate_ref, value_ref), edges)
        at += size


def triangle_kernel(
    count, order, me_ref, middle_gain_ref, gain_ref, output_gate_ref, output_value_ref, *rest
):
    units = len(order)
    right_refs, rest = rest[:units], rest[units:]
    pair_refs, rest = rest[:count], rest[count:]
    out_refs, triangle = rest[-1 - units : -1], rest[-1]
    parts = pair_refs[0].shape[1] // LANES
    left_refs = [rest[n * parts : (n + 1) * parts] for n in range((len(rest) - 1 - units) // parts)]
    left_sizes = [refs[0].shape[0] // output_value_ref.shape[0] for refs in left_refs]
    me = me_ref[0]
    sizes = [ref.shape[0] for ref in pair_refs]
    rows = sum(sizes)
    hidden = output_value_ref.shape[0]
    width = right_refs[0].shape[1]
    span = units * width

    def read_left(h):
        whole = [
            jnp.concatenate([ref[pl.ds(pl.multiple_of(h * size, size), size), :] for ref in refs], axis=1)
            for refs, size in zip(left_refs, left_sizes)
        ]
        return jnp.concatenate(whole, axis=0).astype(NARROW)

    fold = 2 if rows >= 32 and rows % 16 == 0 and 2 * span <= LANES else 1
    deep = rows // fold
    lower = lax.broadcasted_iota(jnp.int32, (deep, fold * span), 1) < span

    def multiply(h, total):
        right = jnp.concatenate([ref[h] for ref in right_refs] * fold, axis=0)
        product = lax.dot_general(read_left(h), right, LAST_BY_LAST, preferred_element_type=WIDE_TYPE)
        if fold == 2:
            product = jnp.where(lower, product[:deep], product[deep:])
        product = product.astype(NARROW).astype(WIDE_TYPE)
        triangle[pl.ds(pl.multiple_of(h * deep, deep), deep), : fold * span] = product
        return total + product

    zeros = jnp.zeros((deep, fold * span), WIDE_TYPE)
    mean_value = lax.fori_loop(0, hidden, multiply, zeros, unroll=16) * (1.0 / hidden)

    def spread(h, total):
        at = pl.multiple_of(h * deep, deep)
        centred = triangle[pl.ds(at, deep), : fold * span] - mean_value
        return total + centred * centred

    variance = lax.fori_loop(0, hidden, spread, zeros, unroll=16) * (1.0 / hidden)
    scale = lax.rsqrt(variance + 1e-05)

    def normalise(h, carry):
        at = pl.multiple_of(h * deep, deep)
        triangle[pl.ds(at, deep), : fold * span] = (
            (triangle[pl.ds(at, deep), : fold * span] - mean_value) * scale * middle_gain_ref[h]
        )
        return carry

    lax.fori_loop(0, hidden, normalise, 0, unroll=16)
    homes = [(ref, i) for ref in pair_refs for i in range(ref.shape[0])]
    columns = [pl.multiple_of((me ^ unit) * width, width) for unit in order]
    for row in range(deep):
        middle = triangle[pl.ds(row, hidden, stride=deep), :].T[: fold * span].astype(NARROW)
        projected = jnp.dot(middle, output_value_ref[...], preferred_element_type=WIDE_TYPE)
        base = jnp.concatenate(
            [
                homes[row + f * deep][0][homes[row + f * deep][1], pl.ds(column, width), :]
                for f in range(fold)
                for column in columns
            ],
            axis=0,
        )
        normed = norm_rows(base, gain_ref[...])
        gating = sigmoid(jnp.dot(normed, output_gate_ref[...], preferred_element_type=WIDE_TYPE))
        updated = (base.astype(WIDE_TYPE) + gating * projected).astype(NARROW)
        for f in range(fold):
            for u in range(units):
                at = (f * units + u) * width
                out_refs[u][row + f * deep] = updated[at : at + width]


def place_kernel(places, base, rows, me_ref, *rest):
    count = len(places)
    in_refs, out_ref, sem = rest[:count], rest[count], rest[count + 1]
    me = me_ref[0]
    copies = []
    for n, (right_unit, parts) in enumerate(places):
        start = 0
        for unit, offset, size in parts:
            at = home_of(me ^ right_unit, unit, base) * rows + offset
            copies.append(
                pltpu.make_async_copy(
                    in_refs[n].at[pl.ds(start, size)], out_ref.at[pl.ds(at, size)], sem.at[len(copies)]
                )
            )
            start += size
    for copy in copies:
        copy.start()
    for copy in copies:
        copy.wait()


def behind(kernel, count):
    def body(*refs):
        kernel(*refs[count:])

    return body


def edge_scratch(rows, hidden, residues):
    return [pltpu.VMEM((hidden * rows, LANES), WIDE_TYPE)] * (residues // LANES)


def edge_call(deps, unit, offset, rows, cost, me, chain, mask, gain, gate, value, pairs, ready=()):
    fresh = sum(p.shape[0] for p in pairs)
    residues = pairs[0].shape[1]
    hidden = gate.shape[1]
    return pl.pallas_call(
        behind(functools.partial(edge_kernel, unit, offset, len(pairs), len(ready)), len(deps)),
        out_shape=jax.ShapeDtypeStruct((hidden, rows, residues), NARROW),
        in_specs=[ANY] * len(deps) + [SMEM] * 2 + [VMEM] * (4 + len(pairs) + len(ready)),
        out_specs=VMEM,
        scratch_shapes=edge_scratch(fresh, hidden, residues),
        compiler_params=pltpu.CompilerParams(vmem_limit_bytes=16 << 20),
        cost_estimate=cost,
        name="edges",
    )(*deps, me, chain, mask, gain, gate, value, *pairs, *ready)


def left_call(deps, unit, base, span, offsets, cost, me, chain, mask, gain, gate, value, pairs):
    rows = sum(p.shape[0] for p in pairs)
    residues = pairs[0].shape[1]
    hidden = gate.shape[1]
    shapes = [jax.ShapeDtypeStruct((hidden * rows, LANES), WIDE_TYPE)] * (residues // LANES)
    return pl.pallas_call(
        behind(functools.partial(left_kernel, unit, base, span, offsets), len(deps)),
        out_shape=shapes,
        in_specs=[ANY] * len(deps) + [SMEM] * 2 + [VMEM] * (4 + len(pairs)),
        out_specs=[VMEM] * len(shapes),
        compiler_params=pltpu.CompilerParams(vmem_limit_bytes=16 << 20),
        cost_estimate=cost,
        name="left_edges",
    )(*deps, me, chain, mask, gain, gate, value, *pairs)


def triangle_call(deps, order, me, middle_gain, gain, output_gate, output_value, right, pairs, lefts):
    _, _, channels = pairs[0].shape
    rows = sum(p.shape[0] for p in pairs)
    hidden = output_value.shape[0]
    width = right[0].shape[1]
    tensors = [gain, output_gate, output_value, *right, *pairs]
    for left in lefts:
        tensors += left
    return pl.pallas_call(
        behind(functools.partial(triangle_kernel, len(pairs), order), len(deps)),
        out_shape=[jax.ShapeDtypeStruct((rows, width, channels), NARROW)] * len(order),
        in_specs=[ANY] * len(deps) + [SMEM] * 2 + [VMEM] * len(tensors),
        out_specs=[VMEM] * len(order),
        scratch_shapes=[pltpu.VMEM((hidden * rows, LANES), WIDE_TYPE)],
        compiler_params=pltpu.CompilerParams(vmem_limit_bytes=40 << 20),
        cost_estimate=pl.CostEstimate(flops=1 << 20, bytes_accessed=1 << 10, transcendentals=0),
        name="triangle",
    )(*deps, me, middle_gain, *tensors)


def place_call(places, base, rows, me, blocks, shape):
    return pl.pallas_call(
        functools.partial(place_kernel, places, base, rows),
        out_shape=jax.ShapeDtypeStruct(shape, NARROW),
        in_specs=[SMEM] + [ANY] * len(blocks),
        out_specs=ANY,
        scratch_shapes=[pltpu.SemaphoreType.DMA((sum(len(parts) for _, parts in places),))],
        compiler_params=pltpu.CompilerParams(vmem_limit_bytes=8 << 20),
        name="place",
    )(me, *blocks)


def hold_kernel(*refs):
    pass


def hold(value, *deps, cost=SHORT):
    return pl.pallas_call(
        hold_kernel,
        out_shape=jax.ShapeDtypeStruct(value.shape, value.dtype),
        in_specs=[ANY] * (1 + len(deps)),
        out_specs=ANY,
        input_output_aliases={0: 0},
        compiler_params=pltpu.CompilerParams(vmem_limit_bytes=1 << 20),
        cost_estimate=cost,
        name="hold",
    )(value, *deps)


def split_kernel(count, in_ref, *rest):
    out_refs, sem = rest[:count], rest[count]
    size = in_ref.shape[0] // count
    copies = [
        pltpu.make_async_copy(in_ref.at[pl.ds(n * size, size)], out_refs[n], sem.at[n]) for n in range(count)
    ]
    for copy in copies:
        copy.start()
    for copy in copies:
        copy.wait()


def split_call(values, count):
    shape = (values.shape[0] // count, *values.shape[1:])
    return pl.pallas_call(
        functools.partial(split_kernel, count),
        out_shape=[jax.ShapeDtypeStruct(shape, values.dtype)] * count,
        in_specs=[ANY],
        out_specs=[VMEM] * count,
        scratch_shapes=[pltpu.SemaphoreType.DMA((count,))],
        compiler_params=pltpu.CompilerParams(vmem_limit_bytes=8 << 20),
        cost_estimate=SHORT,
        name="split",
    )(values)


def make_shards(count):
    bits = [1 << b for b in range(count.bit_length() - 1)]
    near_bit, far_bit, low_bit = bits[0], bits[-1], bits[-2]
    side_bits = bits[1:-2][::-1]
    base = (far_bit, low_bit)

    def swap(values, mask):
        return lax.ppermute(values, "wide", [(d, d ^ mask) for d in range(count)])

    def cross(values):
        inner = lambda d: bool(d & far_bit) != bool(d & low_bit)
        pairs = [(d, d ^ far_bit ^ low_bit if inner(d) else d) for d in range(count)]
        return lax.ppermute(values, "wide", pairs)

    def shards(
        pair,
        residue_mask,
        input_gain,
        left_gate,
        left_value,
        right_gate,
        right_value,
        middle_gain,
        output_gate,
        output_value,
    ):
        rows = pair.shape[0]
        me = lax.axis_index("wide").astype(jnp.int32).reshape(1)
        mask = residue_mask.reshape(1, -1)
        gain = input_gain.reshape(1, -1)
        half = rows // 2
        offsets = (0, half)
        own = split_call(pair, 2)

        def right_edges(deps, unit, offset, raws, ready=(), cost=SHORT):
            return edge_call(
                deps, unit, offset, rows, cost, me, residue_mask, mask, gain, right_gate, right_value, raws, ready
            )

        def piece_edges(weights, shift, deps, unit, at, cost, raws):
            return left_call(
                deps, unit, shift, rows, at, cost, me, residue_mask, mask, gain, *weights, raws
            )

        right_piece = functools.partial(piece_edges, (right_gate, right_value), None)
        left_edges = functools.partial(piece_edges, (left_gate, left_value), base)

        blocks = []
        places = []

        def finish(deps, sources, lefts):
            pairs = [raw for _, _, raw in sources]
            outs = triangle_call(
                deps, order, me, middle_gain, gain, output_gate, output_value, rights, pairs, lefts
            )
            parts = [(unit, offset, raw.shape[0]) for unit, offset, raw in sources]
            for unit, out in zip(order, outs):
                blocks.append(out if unit == 0 else swap(out, unit))
                places.append((unit, parts))
            return outs[0]

        first = cross(pair)
        side = [swap(piece, low_bit) for piece in own]
        right = {0: right_edges((), 0, 0, own)}
        last = right[0]
        plain = {0: own[::-1]}
        for bit in side_bits:
            for unit in list(plain):
                plain[unit ^ bit] = [swap(piece, bit) for piece in plain[unit]]
        others = list(plain)[1:]
        side[0] = hold(side[0], last)
        side_ready = right_piece((last,), low_bit, (0,), SHORT, side[:1])
        last = side_ready[0]
        plain_ready = {}
        for unit in others:
            plain_ready[unit] = right_piece((last,), unit, (half,), SHORT, plain[unit][:1])
            last = plain_ready[unit][0]
        first = hold(first, last)
        left = left_edges((last,), 0, (0,), SHORT, [first])
        last = left[0]
        for unit in others:
            last = right[unit] = right_edges((last,), unit, 0, plain[unit][1:], plain_ready[unit])
        side[1] = hold(side[1], last)
        last = right[low_bit] = right_edges((last,), low_bit, half, side[1:], side_ready, LONG)
        both = {low_bit: side}
        for bit in side_bits:
            for unit in [unit ^ low_bit for unit in both]:
                across = hold(plain[unit ^ bit][0], first)
                there = [swap(both[unit ^ low_bit][0], bit), swap(across, low_bit)]
                both[unit ^ bit ^ low_bit] = there
        second = [cross(piece) for piece in side]
        first_near = swap(first, near_bit)
        left_near = left_edges((last,), near_bit, (0,), SHORT, [first_near])
        last = left_near[0]
        second[0] = hold(second[0], last)
        early = left_edges((), low_bit, (0,), SHORT, second[:1])
        last = early[0]
        for unit in list(both)[1:]:
            last = right[unit] = right_edges((last,), unit, 0, both[unit])
        order = list(right)
        rights = list(right.values())
        early_near = swap(second[0], near_bit)
        left_early = left_edges((last,), low_bit ^ near_bit, (0,), SHORT, [early_near])
        done = finish(
            (),
            [(0, 0, first), (near_bit, 0, first_near), (low_bit, 0, second[0]), (low_bit ^ near_bit, 0, early_near)],
            [left, left_near, early, left_early],
        )

        late_raw = hold(second[1], done)
        late_near = swap(late_raw, near_bit)
        late = left_edges((done,), low_bit, (half,), SHORT, [late_raw])
        left_late = left_edges((late[0],), low_bit ^ near_bit, (half,), SHORT, [late_near])
        finish((), [(low_bit, half, late_raw), (low_bit ^ near_bit, half, late_near)], [late, left_late])
        return place_call(places, base, rows, me, blocks, (count * rows, rows, pair.shape[2]))

    return shards


def solution(mesh):
    in_specs = (P(("groups", "wide"), None, None), P("groups")) + (P(),) * 8
    out_specs = P("groups", "wide", None)
    return jax.shard_map(
        make_shards(mesh.shape["wide"]), mesh=mesh, in_specs=in_specs, out_specs=out_specs, check_vma=False
    )
```

```python
import functools

import jax
import jax.numpy as jnp
from jax import lax
from jax.experimental import pallas as pl
from jax.experimental.pallas import tpu as pltpu
from jax.sharding import PartitionSpec as P

LANES = 128
WIDE_TYPE = jnp.float32
NARROW = jnp.bfloat16
LAST_BY_LAST = (((1,), (1,)), ((), ()))
VMEM = pl.BlockSpec(memory_space=pltpu.VMEM)
SMEM = pl.BlockSpec(memory_space=pltpu.SMEM)
ANY = pl.BlockSpec(memory_space=pl.ANY)


SHORT = pl.CostEstimate(flops=1 << 20, bytes_accessed=1 << 10, transcendentals=0)
LONG = pl.CostEstimate(flops=1 << 35, bytes_accessed=1 << 10, transcendentals=0)


def sigmoid(values):
    return 0.5 * jnp.tanh(0.5 * values) + 0.5


def norm_rows(values, gain):
    values = values.astype(WIDE_TYPE)
    mean_value = jnp.mean(values, axis=1, keepdims=True)
    centred = values - mean_value
    variance = jnp.mean(centred * centred, axis=1, keepdims=True)
    return (centred * lax.rsqrt(variance + 1e-05) * gain).astype(NARROW)


def home_of(me, unit, base):
    far_bit, low_bit = base
    inner = jnp.where((me & far_bit) != 0, 1, 0) ^ jnp.where((me & low_bit) != 0, 1, 0)
    return me ^ unit ^ (inner * (far_bit | low_bit))


def fill_edges(first, at, rows, total, load, chain_ref, mask_ref, gain_ref, weight_refs, edges):
    channels, hidden = weight_refs[0].shape
    gain = jnp.broadcast_to(gain_ref[...], (channels, channels)).T[:, :1]
    weights = jnp.concatenate([ref[...].T for ref in weight_refs], axis=0)
    column_mask = mask_ref[...].astype(WIDE_TYPE)

    def one_row(i, carry):
        values = load(i).T.astype(WIDE_TYPE)
        mean_value = jnp.mean(values, axis=0, keepdims=True)
        centred = values - mean_value
        variance = jnp.mean(centred * centred, axis=0, keepdims=True)
        normed = (centred * lax.rsqrt(variance + 1e-05) * gain).astype(NARROW)
        both = jnp.dot(weights, normed, preferred_element_type=WIDE_TYPE)
        row_mask = chain_ref[first + i].astype(WIDE_TYPE)
        masked = sigmoid(both[:hidden]) * both[hidden:] * (column_mask * row_mask)
        for part in range(len(edges)):
            edges[part][pl.ds(at + i, hidden, stride=total), :] = masked[
                :, part * LANES : (part + 1) * LANES
            ]
        return carry

    lax.fori_loop(0, rows, one_row, 0, unroll=min(rows, 16))


def read_rows(parts, h, size):
    at = pl.ds(pl.multiple_of(h * size, size), size)
    return jnp.concatenate([part[at, :] for part in parts], axis=1)


def edge_kernel(unit, offset, count, ready, me_ref, chain_ref, mask_ref, gain_ref, gate_ref, value_ref, *rest):
    pair_refs, ready_refs, out_ref, edges = rest[:count], rest[count:][:ready], rest[count + ready], rest[count + ready + 1 :]
    rows = out_ref.shape[1]
    fresh = sum(ref.shape[0] for ref in pair_refs)
    at = 0
    for pair_ref in pair_refs:
        size = pair_ref.shape[0]
        first = (me_ref[0] ^ unit) * rows + offset + at
        load = lambda i: pair_ref[i]
        fill_edges(first, at, size, fresh, load, chain_ref, mask_ref, gain_ref, (gate_ref, value_ref), edges)
        at += size

    def one_channel(h, carry):
        pieces = [(offset, read_rows(edges, h, fresh))]
        if ready:
            pieces.append((fresh - offset, read_rows(ready_refs, h, rows - fresh)))
        pieces.sort(key=lambda piece: piece[0])
        out_ref[h] = jnp.concatenate([piece for _, piece in pieces], axis=0).astype(NARROW)
        return carry

    lax.fori_loop(0, out_ref.shape[0], one_channel, 0, unroll=16)


def left_kernel(unit, base, span, offsets, me_ref, chain_ref, mask_ref, gain_ref, gate_ref, value_ref, *rest):
    count = len(offsets)
    pair_refs, edges = rest[:count], rest[count:]
    total = sum(ref.shape[0] for ref in pair_refs)
    at = 0
    for offset, pair_ref in zip(offsets, pair_refs):
        size = pair_ref.shape[0]
        home = me_ref[0] ^ unit if base is None else home_of(me_ref[0], unit, base)
        first = home * span + offset
        load = lambda i: pair_ref[i]
        fill_edges(first, at, size, total, load, chain_ref, mask_ref, gain_ref, (gate_ref, value_ref), edges)
        at += size


def triangle_kernel(
    count, order, me_ref, middle_gain_ref, gain_ref, output_gate_ref, output_value_ref, *rest
):
    units = len(order)
    right_refs, rest = rest[:units], rest[units:]
    pair_refs, rest = rest[:count], rest[count:]
    out_refs, triangle = rest[-1 - units : -1], rest[-1]
    parts = pair_refs[0].shape[1] // LANES
    left_refs = [rest[n * parts : (n + 1) * parts] for n in range((len(rest) - 1 - units) // parts)]
    left_sizes = [refs[0].shape[0] // output_value_ref.shape[0] for refs in left_refs]
    me = me_ref[0]
    sizes = [ref.shape[0] for ref in pair_refs]
    rows = sum(sizes)
    hidden = output_value_ref.shape[0]
    width = right_refs[0].shape[1]
    span = units * width

    def read_left(h):
        whole = [
            jnp.concatenate([ref[pl.ds(pl.multiple_of(h * size, size), size), :] for ref in refs], axis=1)
            for refs, size in zip(left_refs, left_sizes)
        ]
        return jnp.concatenate(whole, axis=0).astype(NARROW)

    fold = 2 if rows >= 32 and rows % 16 == 0 and 2 * span <= LANES else 1
    deep = rows // fold
    lower = lax.broadcasted_iota(jnp.int32, (deep, fold * span), 1) < span

    def multiply(h, total):
        right = jnp.concatenate([ref[h] for ref in right_refs] * fold, axis=0)
        product = lax.dot_general(read_left(h), right, LAST_BY_LAST, preferred_element_type=WIDE_TYPE)
        if fold == 2:
            product = jnp.where(lower, product[:deep], product[deep:])
        product = product.astype(NARROW).astype(WIDE_TYPE)
        triangle[pl.ds(pl.multiple_of(h * deep, deep), deep), : fold * span] = product
        return total + product

    zeros = jnp.zeros((deep, fold * span), WIDE_TYPE)
    mean_value = lax.fori_loop(0, hidden, multiply, zeros, unroll=16) * (1.0 / hidden)

    def spread(h, total):
        at = pl.multiple_of(h * deep, deep)
        centred = triangle[pl.ds(at, deep), : fold * span] - mean_value
        return total + centred * centred

    variance = lax.fori_loop(0, hidden, spread, zeros, unroll=16) * (1.0 / hidden)
    scale = lax.rsqrt(variance + 1e-05)

    def normalise(h, carry):
        at = pl.multiple_of(h * deep, deep)
        triangle[pl.ds(at, deep), : fold * span] = (
            (triangle[pl.ds(at, deep), : fold * span] - mean_value) * scale * middle_gain_ref[h]
        )
        return carry

    lax.fori_loop(0, hidden, normalise, 0, unroll=16)
    homes = [(ref, i) for ref in pair_refs for i in range(ref.shape[0])]
    columns = [pl.multiple_of((me ^ unit) * width, width) for unit in order]
    for row in range(deep):
        middle = triangle[pl.ds(row, hidden, stride=deep), :].astype(NARROW).T[: fold * span]
        projected = jnp.dot(middle, output_value_ref[...], preferred_element_type=WIDE_TYPE)
        base = jnp.concatenate(
            [
                homes[row + f * deep][0][homes[row + f * deep][1], pl.ds(column, width), :]
                for f in range(fold)
                for column in columns
            ],
            axis=0,
        )
        normed = norm_rows(base, gain_ref[...])
        gating = sigmoid(jnp.dot(normed, output_gate_ref[...], preferred_element_type=WIDE_TYPE))
        updated = (base.astype(WIDE_TYPE) + gating * projected).astype(NARROW)
        for f in range(fold):
            for u in range(units):
                at = (f * units + u) * width
                out_refs[u][row + f * deep] = updated[at : at + width]


def place_kernel(places, base, rows, me_ref, *rest):
    count = len(places)
    in_refs, out_ref, sem = rest[:count], rest[count], rest[count + 1]
    me = me_ref[0]
    copies = []
    for n, (right_unit, parts) in enumerate(places):
        start = 0
        for unit, offset, size in parts:
            at = home_of(me ^ right_unit, unit, base) * rows + offset
            copies.append(
                pltpu.make_async_copy(
                    in_refs[n].at[pl.ds(start, size)], out_ref.at[pl.ds(at, size)], sem.at[len(copies)]
                )
            )
            start += size
    for copy in copies:
        copy.start()
    for copy in copies:
        copy.wait()


def behind(kernel, count):
    def body(*refs):
        kernel(*refs[count:])

    return body


def edge_scratch(rows, hidden, residues):
    return [pltpu.VMEM((hidden * rows, LANES), WIDE_TYPE)] * (residues // LANES)


def edge_call(deps, unit, offset, rows, cost, me, chain, mask, gain, gate, value, pairs, ready=()):
    fresh = sum(p.shape[0] for p in pairs)
    residues = pairs[0].shape[1]
    hidden = gate.shape[1]
    return pl.pallas_call(
        behind(functools.partial(edge_kernel, unit, offset, len(pairs), len(ready)), len(deps)),
        out_shape=jax.ShapeDtypeStruct((hidden, rows, residues), NARROW),
        in_specs=[ANY] * len(deps) + [SMEM] * 2 + [VMEM] * (4 + len(pairs) + len(ready)),
        out_specs=VMEM,
        scratch_shapes=edge_scratch(fresh, hidden, residues),
        compiler_params=pltpu.CompilerParams(vmem_limit_bytes=16 << 20),
        cost_estimate=cost,
        name="edges",
    )(*deps, me, chain, mask, gain, gate, value, *pairs, *ready)


def left_call(deps, unit, base, span, offsets, cost, me, chain, mask, gain, gate, value, pairs):
    rows = sum(p.shape[0] for p in pairs)
    residues = pairs[0].shape[1]
    hidden = gate.shape[1]
    shapes = [jax.ShapeDtypeStruct((hidden * rows, LANES), WIDE_TYPE)] * (residues // LANES)
    return pl.pallas_call(
        behind(functools.partial(left_kernel, unit, base, span, offsets), len(deps)),
        out_shape=shapes,
        in_specs=[ANY] * len(deps) + [SMEM] * 2 + [VMEM] * (4 + len(pairs)),
        out_specs=[VMEM] * len(shapes),
        compiler_params=pltpu.CompilerParams(vmem_limit_bytes=16 << 20),
        cost_estimate=cost,
        name="left_edges",
    )(*deps, me, chain, mask, gain, gate, value, *pairs)


def triangle_call(deps, order, me, middle_gain, gain, output_gate, output_value, right, pairs, lefts):
    _, _, channels = pairs[0].shape
    rows = sum(p.shape[0] for p in pairs)
    hidden = output_value.shape[0]
    width = right[0].shape[1]
    tensors = [gain, output_gate, output_value, *right, *pairs]
    for left in lefts:
        tensors += left
    return pl.pallas_call(
        behind(functools.partial(triangle_kernel, len(pairs), order), len(deps)),
        out_shape=[jax.ShapeDtypeStruct((rows, width, channels), NARROW)] * len(order),
        in_specs=[ANY] * len(deps) + [SMEM] * 2 + [VMEM] * len(tensors),
        out_specs=[VMEM] * len(order),
        scratch_shapes=[pltpu.VMEM((hidden * rows, LANES), WIDE_TYPE)],
        compiler_params=pltpu.CompilerParams(vmem_limit_bytes=40 << 20),
        cost_estimate=pl.CostEstimate(flops=1 << 20, bytes_accessed=1 << 10, transcendentals=0),
        name="triangle",
    )(*deps, me, middle_gain, *tensors)


def place_call(places, base, rows, me, blocks, shape):
    return pl.pallas_call(
        functools.partial(place_kernel, places, base, rows),
        out_shape=jax.ShapeDtypeStruct(shape, NARROW),
        in_specs=[SMEM] + [ANY] * len(blocks),
        out_specs=ANY,
        scratch_shapes=[pltpu.SemaphoreType.DMA((sum(len(parts) for _, parts in places),))],
        compiler_params=pltpu.CompilerParams(vmem_limit_bytes=8 << 20),
        name="place",
    )(me, *blocks)


def hold_kernel(*refs):
    pass


def hold(value, *deps, cost=SHORT):
    return pl.pallas_call(
        hold_kernel,
        out_shape=jax.ShapeDtypeStruct(value.shape, value.dtype),
        in_specs=[ANY] * (1 + len(deps)),
        out_specs=ANY,
        input_output_aliases={0: 0},
        compiler_params=pltpu.CompilerParams(vmem_limit_bytes=1 << 20),
        cost_estimate=cost,
        name="hold",
    )(value, *deps)


def split_kernel(count, in_ref, *rest):
    out_refs, sem = rest[:count], rest[count]
    size = in_ref.shape[0] // count
    copies = [
        pltpu.make_async_copy(in_ref.at[pl.ds(n * size, size)], out_refs[n], sem.at[n]) for n in range(count)
    ]
    for copy in copies:
        copy.start()
    for copy in copies:
        copy.wait()


def split_call(values, count):
    shape = (values.shape[0] // count, *values.shape[1:])
    return pl.pallas_call(
        functools.partial(split_kernel, count),
        out_shape=[jax.ShapeDtypeStruct(shape, values.dtype)] * count,
        in_specs=[ANY],
        out_specs=[VMEM] * count,
        scratch_shapes=[pltpu.SemaphoreType.DMA((count,))],
        compiler_params=pltpu.CompilerParams(vmem_limit_bytes=8 << 20),
        cost_estimate=SHORT,
        name="split",
    )(values)


def make_shards(count):
    bits = [1 << b for b in range(count.bit_length() - 1)]
    near_bit, far_bit, low_bit = bits[0], bits[-1], bits[-2]
    side_bits = bits[1:-2][::-1]
    base = (far_bit, low_bit)

    def swap(values, mask):
        return lax.ppermute(values, "wide", [(d, d ^ mask) for d in range(count)])

    def cross(values):
        inner = lambda d: bool(d & far_bit) != bool(d & low_bit)
        pairs = [(d, d ^ far_bit ^ low_bit if inner(d) else d) for d in range(count)]
        return lax.ppermute(values, "wide", pairs)

    def shards(
        pair,
        residue_mask,
        input_gain,
        left_gate,
        left_value,
        right_gate,
        right_value,
        middle_gain,
        output_gate,
        output_value,
    ):
        rows = pair.shape[0]
        me = lax.axis_index("wide").astype(jnp.int32).reshape(1)
        mask = residue_mask.reshape(1, -1)
        gain = input_gain.reshape(1, -1)
        half = rows // 2
        offsets = (0, half)
        own = split_call(pair, 2)

        def right_edges(deps, unit, offset, raws, ready=(), cost=SHORT):
            return edge_call(
                deps, unit, offset, rows, cost, me, residue_mask, mask, gain, right_gate, right_value, raws, ready
            )

        def piece_edges(weights, shift, deps, unit, at, cost, raws):
            return left_call(
                deps, unit, shift, rows, at, cost, me, residue_mask, mask, gain, *weights, raws
            )

        right_piece = functools.partial(piece_edges, (right_gate, right_value), None)
        left_edges = functools.partial(piece_edges, (left_gate, left_value), base)

        blocks = []
        places = []

        def finish(deps, sources, lefts):
            pairs = [raw for _, _, raw in sources]
            outs = triangle_call(
                deps, order, me, middle_gain, gain, output_gate, output_value, rights, pairs, lefts
            )
            parts = [(unit, offset, raw.shape[0]) for unit, offset, raw in sources]
            for unit, out in zip(order, outs):
                blocks.append(out if unit == 0 else swap(out, unit))
                places.append((unit, parts))
            return outs[0]

        first = cross(pair)
        side = [swap(piece, low_bit) for piece in own]
        right = {0: right_edges((), 0, 0, own)}
        last = right[0]
        plain = {0: own[::-1]}
        for bit in side_bits:
            for unit in list(plain):
                plain[unit ^ bit] = [swap(piece, bit) for piece in plain[unit]]
        others = list(plain)[1:]
        side[0] = hold(side[0], last)
        side_ready = right_piece((last,), low_bit, (0,), SHORT, side[:1])
        last = side_ready[0]
        plain_ready = {}
        for unit in others:
            plain_ready[unit] = right_piece((last,), unit, (half,), SHORT, plain[unit][:1])
            last = plain_ready[unit][0]
        first = hold(first, last)
        left = left_edges((last,), 0, (0,), SHORT, [first])
        last = left[0]
        for unit in others:
            last = right[unit] = right_edges((last,), unit, 0, plain[unit][1:], plain_ready[unit])
        side[1] = hold(side[1], last)
        last = right[low_bit] = right_edges((last,), low_bit, half, side[1:], side_ready, LONG)
        both = {low_bit: side}
        for bit in side_bits:
            for unit in [unit ^ low_bit for unit in both]:
                across = hold(plain[unit ^ bit][0], first)
                there = [swap(both[unit ^ low_bit][0], bit), swap(across, low_bit)]
                both[unit ^ bit ^ low_bit] = there
        second = [cross(piece) for piece in side]
        first_near = swap(first, near_bit)
        left_near = left_edges((last,), near_bit, (0,), SHORT, [first_near])
        last = left_near[0]
        second[0] = hold(second[0], last)
        early = left_edges((), low_bit, (0,), SHORT, second[:1])
        last = early[0]
        for unit in list(both)[1:]:
            last = right[unit] = right_edges((last,), unit, 0, both[unit])
        order = [0] + list(right)[:0:-1]
        rights = [right[unit] for unit in order]
        early_near = swap(second[0], near_bit)
        left_early = left_edges((last,), low_bit ^ near_bit, (0,), SHORT, [early_near])
        done = finish(
            (),
            [(0, 0, first), (near_bit, 0, first_near), (low_bit, 0, second[0]), (low_bit ^ near_bit, 0, early_near)],
            [left, left_near, early, left_early],
        )

        late_raw = hold(second[1], done)
        late_near = swap(late_raw, near_bit)
        late = left_edges((done,), low_bit, (half,), SHORT, [late_raw])
        left_late = left_edges((late[0],), low_bit ^ near_bit, (half,), SHORT, [late_near])
        finish((), [(low_bit, half, late_raw), (low_bit ^ near_bit, half, late_near)], [late, left_late])
        return place_call(places, base, rows, me, blocks, (count * rows, rows, pair.shape[2]))

    return shards


def solution(mesh):
    in_specs = (P(("groups", "wide"), None, None), P("groups")) + (P(),) * 8
    out_specs = P("groups", "wide", None)
    return jax.shard_map(
        make_shards(mesh.shape["wide"]), mesh=mesh, in_specs=in_specs, out_specs=out_specs, check_vma=False
    )
```

```python
import functools

import jax
import jax.numpy as jnp
from jax import lax
from jax.experimental import pallas as pl
from jax.experimental.pallas import tpu as pltpu
from jax.sharding import PartitionSpec as P

LANES = 128
WIDE_TYPE = jnp.float32
NARROW = jnp.bfloat16
LAST_BY_LAST = (((1,), (1,)), ((), ()))
VMEM = pl.BlockSpec(memory_space=pltpu.VMEM)
SMEM = pl.BlockSpec(memory_space=pltpu.SMEM)
ANY = pl.BlockSpec(memory_space=pl.ANY)


SHORT = pl.CostEstimate(flops=1 << 20, bytes_accessed=1 << 10, transcendentals=0)
LONG = pl.CostEstimate(flops=1 << 35, bytes_accessed=1 << 10, transcendentals=0)


def sigmoid(values):
    return 0.5 * jnp.tanh(0.5 * values) + 0.5


def norm_rows(values, gain):
    values = values.astype(WIDE_TYPE)
    mean_value = jnp.mean(values, axis=1, keepdims=True)
    centred = values - mean_value
    variance = jnp.mean(centred * centred, axis=1, keepdims=True)
    return (centred * lax.rsqrt(variance + 1e-05) * gain).astype(NARROW)


def home_of(me, unit, base):
    far_bit, low_bit = base
    inner = jnp.where((me & far_bit) != 0, 1, 0) ^ jnp.where((me & low_bit) != 0, 1, 0)
    return me ^ unit ^ (inner * (far_bit | low_bit))


def fill_edges(first, at, rows, total, load, chain_ref, mask_ref, gain_ref, weight_refs, edges):
    channels, hidden = weight_refs[0].shape
    gain = jnp.broadcast_to(gain_ref[...], (channels, channels)).T[:, :1]
    weights = jnp.concatenate([ref[...].T for ref in weight_refs], axis=0)
    column_mask = mask_ref[...].astype(WIDE_TYPE)

    def one_row(i, carry):
        values = load(i).T.astype(WIDE_TYPE)
        mean_value = jnp.mean(values, axis=0, keepdims=True)
        centred = values - mean_value
        variance = jnp.mean(centred * centred, axis=0, keepdims=True)
        normed = (centred * lax.rsqrt(variance + 1e-05) * gain).astype(NARROW)
        both = jnp.dot(weights, normed, preferred_element_type=WIDE_TYPE)
        row_mask = chain_ref[first + i].astype(WIDE_TYPE)
        masked = sigmoid(both[:hidden]) * both[hidden:] * (column_mask * row_mask)
        for part in range(len(edges)):
            edges[part][pl.ds(at + i, hidden, stride=total), :] = masked[
                :, part * LANES : (part + 1) * LANES
            ]
        return carry

    lax.fori_loop(0, rows, one_row, 0, unroll=min(rows, 16))


def read_rows(parts, h, size):
    at = pl.ds(pl.multiple_of(h * size, size), size)
    return jnp.concatenate([part[at, :] for part in parts], axis=1)


def edge_kernel(unit, offset, count, ready, me_ref, chain_ref, mask_ref, gain_ref, gate_ref, value_ref, *rest):
    pair_refs, ready_refs, out_ref, edges = rest[:count], rest[count:][:ready], rest[count + ready], rest[count + ready + 1 :]
    rows = out_ref.shape[1]
    fresh = sum(ref.shape[0] for ref in pair_refs)
    at = 0
    for pair_ref in pair_refs:
        size = pair_ref.shape[0]
        first = (me_ref[0] ^ unit) * rows + offset + at
        load = lambda i: pair_ref[i]
        fill_edges(first, at, size, fresh, load, chain_ref, mask_ref, gain_ref, (gate_ref, value_ref), edges)
        at += size

    def one_channel(h, carry):
        pieces = [(offset, read_rows(edges, h, fresh))]
        if ready:
            pieces.append((fresh - offset, read_rows(ready_refs, h, rows - fresh)))
        pieces.sort(key=lambda piece: piece[0])
        out_ref[h] = jnp.concatenate([piece for _, piece in pieces], axis=0).astype(NARROW)
        return carry

    lax.fori_loop(0, out_ref.shape[0], one_channel, 0, unroll=16)


def left_kernel(unit, base, span, offsets, me_ref, chain_ref, mask_ref, gain_ref, gate_ref, value_ref, *rest):
    count = len(offsets)
    pair_refs, edges = rest[:count], rest[count:]
    total = sum(ref.shape[0] for ref in pair_refs)
    at = 0
    for offset, pair_ref in zip(offsets, pair_refs):
        size = pair_ref.shape[0]
        home = me_ref[0] ^ unit if base is None else home_of(me_ref[0], unit, base)
        first = home * span + offset
        load = lambda i: pair_ref[i]
        fill_edges(first, at, size, total, load, chain_ref, mask_ref, gain_ref, (gate_ref, value_ref), edges)
        at += size


def triangle_kernel(
    count, order, me_ref, middle_gain_ref, gain_ref, output_gate_ref, output_value_ref, *rest
):
    units = len(order)
    right_refs, rest = rest[:units], rest[units:]
    pair_refs, rest = rest[:count], rest[count:]
    out_refs, triangle = rest[-1 - units : -1], rest[-1]
    parts = pair_refs[0].shape[1] // LANES
    left_refs = [rest[n * parts : (n + 1) * parts] for n in range((len(rest) - 1 - units) // parts)]
    left_sizes = [refs[0].shape[0] // output_value_ref.shape[0] for refs in left_refs]
    me = me_ref[0]
    sizes = [ref.shape[0] for ref in pair_refs]
    rows = sum(sizes)
    hidden = output_value_ref.shape[0]
    width = right_refs[0].shape[1]
    span = units * width

    def read_left(h):
        whole = [
            jnp.concatenate([ref[pl.ds(pl.multiple_of(h * size, size), size), :] for ref in refs], axis=1)
            for refs, size in zip(left_refs, left_sizes)
        ]
        return jnp.concatenate(whole, axis=0).astype(NARROW)

    fold = 2 if rows >= 32 and rows % 16 == 0 and 2 * span <= LANES else 1
    deep = rows // fold
    lower = lax.broadcasted_iota(jnp.int32, (deep, fold * span), 1) < span

    def multiply(h, total):
        right = jnp.concatenate([ref[h] for ref in right_refs] * fold, axis=0)
        product = lax.dot_general(read_left(h), right, LAST_BY_LAST, preferred_element_type=WIDE_TYPE)
        if fold == 2:
            product = jnp.where(lower, product[:deep], product[deep:])
        product = product.astype(NARROW).astype(WIDE_TYPE)
        triangle[pl.ds(pl.multiple_of(h * deep, deep), deep), : fold * span] = product
        return total + product

    zeros = jnp.zeros((deep, fold * span), WIDE_TYPE)
    mean_value = lax.fori_loop(0, hidden, multiply, zeros, unroll=16) * (1.0 / hidden)

    def spread(h, total):
        at = pl.multiple_of(h * deep, deep)
        centred = triangle[pl.ds(at, deep), : fold * span] - mean_value
        return total + centred * centred

    variance = lax.fori_loop(0, hidden, spread, zeros, unroll=16) * (1.0 / hidden)
    scale = lax.rsqrt(variance + 1e-05)

    def normalise(h, carry):
        at = pl.multiple_of(h * deep, deep)
        triangle[pl.ds(at, deep), : fold * span] = (
            (triangle[pl.ds(at, deep), : fold * span] - mean_value) * scale * middle_gain_ref[h]
        )
        return carry

    lax.fori_loop(0, hidden, normalise, 0, unroll=16)
    homes = [(ref, i) for ref in pair_refs for i in range(ref.shape[0])]
    columns = [pl.multiple_of((me ^ unit) * width, width) for unit in order]
    for row in range(deep):
        middle = triangle[pl.ds(row, hidden, stride=deep), :].astype(NARROW).T[: fold * span]
        projected = jnp.dot(middle, output_value_ref[...], preferred_element_type=WIDE_TYPE)
        base = jnp.concatenate(
            [
                homes[row + f * deep][0][homes[row + f * deep][1], pl.ds(column, width), :]
                for f in range(fold)
                for column in columns
            ],
            axis=0,
        )
        normed = norm_rows(base, gain_ref[...])
        gating = sigmoid(jnp.dot(normed, output_gate_ref[...], preferred_element_type=WIDE_TYPE))
        updated = (base.astype(WIDE_TYPE) + gating * projected).astype(NARROW)
        for f in range(fold):
            for u in range(units):
                at = (f * units + u) * width
                out_refs[u][row + f * deep] = updated[at : at + width]


def place_kernel(places, base, rows, me_ref, *rest):
    count = len(places)
    in_refs, out_ref, sem = rest[:count], rest[count], rest[count + 1]
    me = me_ref[0]
    copies = []
    for n, (right_unit, parts) in enumerate(places):
        start = 0
        for unit, offset, size in parts:
            at = home_of(me ^ right_unit, unit, base) * rows + offset
            copies.append(
                pltpu.make_async_copy(
                    in_refs[n].at[pl.ds(start, size)], out_ref.at[pl.ds(at, size)], sem.at[len(copies)]
                )
            )
            start += size
    for copy in copies:
        copy.start()
    for copy in copies:
        copy.wait()


def behind(kernel, count):
    def body(*refs):
        kernel(*refs[count:])

    return body


def edge_scratch(rows, hidden, residues):
    return [pltpu.VMEM((hidden * rows, LANES), WIDE_TYPE)] * (residues // LANES)


def edge_call(deps, unit, offset, rows, cost, me, chain, mask, gain, gate, value, pairs, ready=()):
    fresh = sum(p.shape[0] for p in pairs)
    residues = pairs[0].shape[1]
    hidden = gate.shape[1]
    return pl.pallas_call(
        behind(functools.partial(edge_kernel, unit, offset, len(pairs), len(ready)), len(deps)),
        out_shape=jax.ShapeDtypeStruct((hidden, rows, residues), NARROW),
        in_specs=[ANY] * len(deps) + [SMEM] * 2 + [VMEM] * (4 + len(pairs) + len(ready)),
        out_specs=VMEM,
        scratch_shapes=edge_scratch(fresh, hidden, residues),
        compiler_params=pltpu.CompilerParams(vmem_limit_bytes=16 << 20),
        cost_estimate=cost,
        name="edges",
    )(*deps, me, chain, mask, gain, gate, value, *pairs, *ready)


def left_call(deps, unit, base, span, offsets, cost, me, chain, mask, gain, gate, value, pairs):
    rows = sum(p.shape[0] for p in pairs)
    residues = pairs[0].shape[1]
    hidden = gate.shape[1]
    shapes = [jax.ShapeDtypeStruct((hidden * rows, LANES), WIDE_TYPE)] * (residues // LANES)
    return pl.pallas_call(
        behind(functools.partial(left_kernel, unit, base, span, offsets), len(deps)),
        out_shape=shapes,
        in_specs=[ANY] * len(deps) + [SMEM] * 2 + [VMEM] * (4 + len(pairs)),
        out_specs=[VMEM] * len(shapes),
        compiler_params=pltpu.CompilerParams(vmem_limit_bytes=16 << 20),
        cost_estimate=cost,
        name="left_edges",
    )(*deps, me, chain, mask, gain, gate, value, *pairs)


def triangle_call(deps, order, me, middle_gain, gain, output_gate, output_value, right, pairs, lefts):
    _, _, channels = pairs[0].shape
    rows = sum(p.shape[0] for p in pairs)
    hidden = output_value.shape[0]
    width = right[0].shape[1]
    tensors = [gain, output_gate, output_value, *right, *pairs]
    for left in lefts:
        tensors += left
    return pl.pallas_call(
        behind(functools.partial(triangle_kernel, len(pairs), order), len(deps)),
        out_shape=[jax.ShapeDtypeStruct((rows, width, channels), NARROW)] * len(order),
        in_specs=[ANY] * len(deps) + [SMEM] * 2 + [VMEM] * len(tensors),
        out_specs=[VMEM] * len(order),
        scratch_shapes=[pltpu.VMEM((hidden * rows, LANES), WIDE_TYPE)],
        compiler_params=pltpu.CompilerParams(vmem_limit_bytes=40 << 20),
        cost_estimate=pl.CostEstimate(flops=1 << 20, bytes_accessed=1 << 10, transcendentals=0),
        name="triangle",
    )(*deps, me, middle_gain, *tensors)


def place_call(places, base, rows, me, blocks, shape):
    return pl.pallas_call(
        functools.partial(place_kernel, places, base, rows),
        out_shape=jax.ShapeDtypeStruct(shape, NARROW),
        in_specs=[SMEM] + [ANY] * len(blocks),
        out_specs=ANY,
        scratch_shapes=[pltpu.SemaphoreType.DMA((sum(len(parts) for _, parts in places),))],
        compiler_params=pltpu.CompilerParams(vmem_limit_bytes=8 << 20),
        name="place",
    )(me, *blocks)


def hold_kernel(*refs):
    pass


def hold(value, *deps, cost=SHORT):
    return pl.pallas_call(
        hold_kernel,
        out_shape=jax.ShapeDtypeStruct(value.shape, value.dtype),
        in_specs=[ANY] * (1 + len(deps)),
        out_specs=ANY,
        input_output_aliases={0: 0},
        compiler_params=pltpu.CompilerParams(vmem_limit_bytes=1 << 20),
        cost_estimate=cost,
        name="hold",
    )(value, *deps)


def split_kernel(count, in_ref, *rest):
    out_refs, sem = rest[:count], rest[count]
    size = in_ref.shape[0] // count
    copies = [
        pltpu.make_async_copy(in_ref.at[pl.ds(n * size, size)], out_refs[n], sem.at[n]) for n in range(count)
    ]
    for copy in copies:
        copy.start()
    for copy in copies:
        copy.wait()


def split_call(values, count):
    shape = (values.shape[0] // count, *values.shape[1:])
    return pl.pallas_call(
        functools.partial(split_kernel, count),
        out_shape=[jax.ShapeDtypeStruct(shape, values.dtype)] * count,
        in_specs=[ANY],
        out_specs=[VMEM] * count,
        scratch_shapes=[pltpu.SemaphoreType.DMA((count,))],
        compiler_params=pltpu.CompilerParams(vmem_limit_bytes=8 << 20),
        cost_estimate=SHORT,
        name="split",
    )(values)


def make_shards(count):
    bits = [1 << b for b in range(count.bit_length() - 1)]
    near_bit, far_bit, low_bit = bits[0], bits[-1], bits[-2]
    side_bits = bits[1:-2][::-1]
    base = (far_bit, low_bit)

    def swap(values, mask):
        return lax.ppermute(values, "wide", [(d, d ^ mask) for d in range(count)])

    def cross(values):
        inner = lambda d: bool(d & far_bit) != bool(d & low_bit)
        pairs = [(d, d ^ far_bit ^ low_bit if inner(d) else d) for d in range(count)]
        return lax.ppermute(values, "wide", pairs)

    def shards(
        pair,
        residue_mask,
        input_gain,
        left_gate,
        left_value,
        right_gate,
        right_value,
        middle_gain,
        output_gate,
        output_value,
    ):
        rows = pair.shape[0]
        me = lax.axis_index("wide").astype(jnp.int32).reshape(1)
        mask = residue_mask.reshape(1, -1)
        gain = input_gain.reshape(1, -1)
        half = rows // 2
        offsets = (0, half)
        own = split_call(pair, 2)

        def right_edges(deps, unit, offset, raws, ready=(), cost=SHORT):
            return edge_call(
                deps, unit, offset, rows, cost, me, residue_mask, mask, gain, right_gate, right_value, raws, ready
            )

        def piece_edges(weights, shift, deps, unit, at, cost, raws):
            return left_call(
                deps, unit, shift, rows, at, cost, me, residue_mask, mask, gain, *weights, raws
            )

        right_piece = functools.partial(piece_edges, (right_gate, right_value), None)
        left_edges = functools.partial(piece_edges, (left_gate, left_value), base)

        blocks = []
        places = []

        def finish(deps, sources, lefts):
            pairs = [raw for _, _, raw in sources]
            outs = triangle_call(
                deps, order, me, middle_gain, gain, output_gate, output_value, rights, pairs, lefts
            )
            parts = [(unit, offset, raw.shape[0]) for unit, offset, raw in sources]
            for unit, out in zip(order, outs):
                blocks.append(out if unit == 0 else swap(out, unit))
                places.append((unit, parts))
            return outs[0]

        first = cross(pair)
        side = [swap(piece, low_bit) for piece in own]
        right = {0: right_edges((), 0, 0, own)}
        last = right[0]
        plain = {0: own[::-1]}
        for bit in side_bits:
            for unit in list(plain):
                plain[unit ^ bit] = [swap(piece, bit) for piece in plain[unit]]
        others = list(plain)[1:]
        side[0] = hold(side[0], last)
        side_ready = right_piece((last,), low_bit, (0,), SHORT, side[:1])
        last = side_ready[0]
        plain_ready = {}
        for unit in others:
            plain_ready[unit] = right_piece((last,), unit, (half,), SHORT, plain[unit][:1])
            last = plain_ready[unit][0]
        first = hold(first, last)
        left = left_edges((last,), 0, (0,), SHORT, [first])
        last = left[0]
        for unit in others:
            last = right[unit] = right_edges((last,), unit, 0, plain[unit][1:], plain_ready[unit])
        side[1] = hold(side[1], last)
        last = right[low_bit] = right_edges((last,), low_bit, half, side[1:], side_ready, LONG)
        both = {low_bit: side}
        for bit in side_bits:
            for unit in [unit ^ low_bit for unit in both]:
                across = hold(plain[unit ^ bit][0], plain_ready[unit ^ bit][0])
                there = [swap(both[unit ^ low_bit][0], bit), swap(across, low_bit)]
                both[unit ^ bit ^ low_bit] = there
        second = [cross(piece) for piece in side]
        first_near = swap(first, near_bit)
        left_near = left_edges((last,), near_bit, (0,), SHORT, [first_near])
        last = left_near[0]
        second[0] = hold(second[0], last)
        early = left_edges((), low_bit, (0,), SHORT, second[:1])
        last = early[0]
        for unit in list(both)[1:]:
            last = right[unit] = right_edges((last,), unit, 0, both[unit])
        order = [0] + list(right)[:0:-1]
        rights = [right[unit] for unit in order]
        early_near = swap(second[0], near_bit)
        left_early = left_edges((last,), low_bit ^ near_bit, (0,), SHORT, [early_near])
        done = finish(
            (),
            [(0, 0, first), (near_bit, 0, first_near), (low_bit, 0, second[0]), (low_bit ^ near_bit, 0, early_near)],
            [left, left_near, early, left_early],
        )

        late_raw = hold(second[1], done)
        late_near = swap(late_raw, near_bit)
        late = left_edges((done,), low_bit, (half,), SHORT, [late_raw])
        left_late = left_edges((late[0],), low_bit ^ near_bit, (half,), SHORT, [late_near])
        finish((), [(low_bit, half, late_raw), (low_bit ^ near_bit, half, late_near)], [late, left_late])
        return place_call(places, base, rows, me, blocks, (count * rows, rows, pair.shape[2]))

    return shards


def solution(mesh):
    in_specs = (P(("groups", "wide"), None, None), P("groups")) + (P(),) * 8
    out_specs = P("groups", "wide", None)
    return jax.shard_map(
        make_shards(mesh.shape["wide"]), mesh=mesh, in_specs=in_specs, out_specs=out_specs, check_vma=False
    )
```

```python
import functools

import jax
import jax.numpy as jnp
from jax import lax
from jax.experimental import pallas as pl
from jax.experimental.pallas import tpu as pltpu
from jax.sharding import PartitionSpec as P

LANES = 128
WIDE_TYPE = jnp.float32
NARROW = jnp.bfloat16
LAST_BY_LAST = (((1,), (1,)), ((), ()))
VMEM = pl.BlockSpec(memory_space=pltpu.VMEM)
SMEM = pl.BlockSpec(memory_space=pltpu.SMEM)
ANY = pl.BlockSpec(memory_space=pl.ANY)


SHORT = pl.CostEstimate(flops=1 << 20, bytes_accessed=1 << 10, transcendentals=0)
LONG = pl.CostEstimate(flops=1 << 35, bytes_accessed=1 << 10, transcendentals=0)


def sigmoid(values):
    return 0.5 * jnp.tanh(0.5 * values) + 0.5


def norm_rows(values, gain):
    values = values.astype(WIDE_TYPE)
    mean_value = jnp.mean(values, axis=1, keepdims=True)
    centred = values - mean_value
    variance = jnp.mean(centred * centred, axis=1, keepdims=True)
    return (centred * lax.rsqrt(variance + 1e-05) * gain).astype(NARROW)


def home_of(me, unit, base):
    far_bit, low_bit = base
    inner = jnp.where((me & far_bit) != 0, 1, 0) ^ jnp.where((me & low_bit) != 0, 1, 0)
    return me ^ unit ^ (inner * (far_bit | low_bit))


def fill_edges(first, at, rows, total, load, chain_ref, mask_ref, gain_ref, weight_refs, edges):
    channels, hidden = weight_refs[0].shape
    gain = jnp.broadcast_to(gain_ref[...], (channels, channels)).T[:, :1]
    weights = jnp.concatenate([ref[...].T for ref in weight_refs], axis=0)
    column_mask = mask_ref[...].astype(WIDE_TYPE)

    def one_row(i, carry):
        values = load(i).T.astype(WIDE_TYPE)
        mean_value = jnp.mean(values, axis=0, keepdims=True)
        centred = values - mean_value
        variance = jnp.mean(centred * centred, axis=0, keepdims=True)
        normed = (centred * lax.rsqrt(variance + 1e-05) * gain).astype(NARROW)
        both = jnp.dot(weights, normed, preferred_element_type=WIDE_TYPE)
        row_mask = chain_ref[first + i].astype(WIDE_TYPE)
        masked = sigmoid(both[:hidden]) * both[hidden:] * (column_mask * row_mask)
        for part in range(len(edges)):
            edges[part][pl.ds(at + i, hidden, stride=total), :] = masked[
                :, part * LANES : (part + 1) * LANES
            ]
        return carry

    lax.fori_loop(0, rows, one_row, 0, unroll=min(rows, 16))


def read_rows(parts, h, size):
    at = pl.ds(pl.multiple_of(h * size, size), size)
    return jnp.concatenate([part[at, :] for part in parts], axis=1)


def edge_kernel(unit, offset, count, ready, me_ref, chain_ref, mask_ref, gain_ref, gate_ref, value_ref, *rest):
    pair_refs, ready_refs, out_ref, edges = rest[:count], rest[count:][:ready], rest[count + ready], rest[count + ready + 1 :]
    rows = out_ref.shape[1]
    fresh = sum(ref.shape[0] for ref in pair_refs)
    at = 0
    for pair_ref in pair_refs:
        size = pair_ref.shape[0]
        first = (me_ref[0] ^ unit) * rows + offset + at
        load = lambda i: pair_ref[i]
        fill_edges(first, at, size, fresh, load, chain_ref, mask_ref, gain_ref, (gate_ref, value_ref), edges)
        at += size

    def one_channel(h, carry):
        pieces = [(offset, read_rows(edges, h, fresh))]
        if ready:
            pieces.append((fresh - offset, read_rows(ready_refs, h, rows - fresh)))
        pieces.sort(key=lambda piece: piece[0])
        out_ref[h] = jnp.concatenate([piece for _, piece in pieces], axis=0).astype(NARROW)
        return carry

    lax.fori_loop(0, out_ref.shape[0], one_channel, 0, unroll=16)


def left_kernel(unit, base, span, offsets, me_ref, chain_ref, mask_ref, gain_ref, gate_ref, value_ref, *rest):
    count = len(offsets)
    pair_refs, edges = rest[:count], rest[count:]
    total = sum(ref.shape[0] for ref in pair_refs)
    at = 0
    for offset, pair_ref in zip(offsets, pair_refs):
        size = pair_ref.shape[0]
        home = me_ref[0] ^ unit if base is None else home_of(me_ref[0], unit, base)
        first = home * span + offset
        load = lambda i: pair_ref[i]
        fill_edges(first, at, size, total, load, chain_ref, mask_ref, gain_ref, (gate_ref, value_ref), edges)
        at += size


def triangle_kernel(
    count, order, me_ref, middle_gain_ref, gain_ref, output_gate_ref, output_value_ref, *rest
):
    units = len(order)
    right_refs, rest = rest[:units], rest[units:]
    pair_refs, rest = rest[:count], rest[count:]
    out_refs, triangle = rest[-1 - units : -1], rest[-1]
    parts = pair_refs[0].shape[1] // LANES
    left_refs = [rest[n * parts : (n + 1) * parts] for n in range((len(rest) - 1 - units) // parts)]
    left_sizes = [refs[0].shape[0] // output_value_ref.shape[0] for refs in left_refs]
    me = me_ref[0]
    sizes = [ref.shape[0] for ref in pair_refs]
    rows = sum(sizes)
    hidden = output_value_ref.shape[0]
    width = right_refs[0].shape[1]
    span = units * width

    def read_left(h):
        whole = [
            jnp.concatenate([ref[pl.ds(pl.multiple_of(h * size, size), size), :] for ref in refs], axis=1)
            for refs, size in zip(left_refs, left_sizes)
        ]
        return jnp.concatenate(whole, axis=0).astype(NARROW)

    fold = 2 if rows >= 32 and rows % 16 == 0 and 2 * span <= LANES else 1
    deep = rows // fold
    lower = lax.broadcasted_iota(jnp.int32, (deep, fold * span), 1) < span

    def multiply(h, total):
        right = jnp.concatenate([ref[h] for ref in right_refs] * fold, axis=0)
        product = lax.dot_general(read_left(h), right, LAST_BY_LAST, preferred_element_type=WIDE_TYPE)
        if fold == 2:
            product = jnp.where(lower, product[:deep], product[deep:])
        product = product.astype(NARROW).astype(WIDE_TYPE)
        triangle[pl.ds(pl.multiple_of(h * deep, deep), deep), : fold * span] = product
        return total + product

    zeros = jnp.zeros((deep, fold * span), WIDE_TYPE)
    mean_value = lax.fori_loop(0, hidden, multiply, zeros, unroll=64) * (1.0 / hidden)

    def spread(h, total):
        at = pl.multiple_of(h * deep, deep)
        centred = triangle[pl.ds(at, deep), : fold * span] - mean_value
        return total + centred * centred

    variance = lax.fori_loop(0, hidden, spread, zeros, unroll=16) * (1.0 / hidden)
    scale = lax.rsqrt(variance + 1e-05)

    def normalise(h, carry):
        at = pl.multiple_of(h * deep, deep)
        triangle[pl.ds(at, deep), : fold * span] = (
            (triangle[pl.ds(at, deep), : fold * span] - mean_value) * scale * middle_gain_ref[h]
        )
        return carry

    lax.fori_loop(0, hidden, normalise, 0, unroll=16)
    homes = [(ref, i) for ref in pair_refs for i in range(ref.shape[0])]
    columns = [pl.multiple_of((me ^ unit) * width, width) for unit in order]
    for row in range(deep):
        middle = triangle[pl.ds(row, hidden, stride=deep), :].astype(NARROW).T[: fold * span]
        projected = jnp.dot(middle, output_value_ref[...], preferred_element_type=WIDE_TYPE)
        base = jnp.concatenate(
            [
                homes[row + f * deep][0][homes[row + f * deep][1], pl.ds(column, width), :]
                for f in range(fold)
                for column in columns
            ],
            axis=0,
        )
        normed = norm_rows(base, gain_ref[...])
        gating = sigmoid(jnp.dot(normed, output_gate_ref[...], preferred_element_type=WIDE_TYPE))
        updated = (base.astype(WIDE_TYPE) + gating * projected).astype(NARROW)
        for f in range(fold):
            for u in range(units):
                at = (f * units + u) * width
                out_refs[u][row + f * deep] = updated[at : at + width]


def place_kernel(places, base, rows, me_ref, *rest):
    count = len(places)
    in_refs, out_ref, sem = rest[:count], rest[count], rest[count + 1]
    me = me_ref[0]
    copies = []
    for n, (right_unit, parts) in enumerate(places):
        start = 0
        for unit, offset, size in parts:
            at = home_of(me ^ right_unit, unit, base) * rows + offset
            copies.append(
                pltpu.make_async_copy(
                    in_refs[n].at[pl.ds(start, size)], out_ref.at[pl.ds(at, size)], sem.at[len(copies)]
                )
            )
            start += size
    for copy in copies:
        copy.start()
    for copy in copies:
        copy.wait()


def behind(kernel, count):
    def body(*refs):
        kernel(*refs[count:])

    return body


def edge_scratch(rows, hidden, residues):
    return [pltpu.VMEM((hidden * rows, LANES), WIDE_TYPE)] * (residues // LANES)


def edge_call(deps, unit, offset, rows, cost, me, chain, mask, gain, gate, value, pairs, ready=()):
    fresh = sum(p.shape[0] for p in pairs)
    residues = pairs[0].shape[1]
    hidden = gate.shape[1]
    return pl.pallas_call(
        behind(functools.partial(edge_kernel, unit, offset, len(pairs), len(ready)), len(deps)),
        out_shape=jax.ShapeDtypeStruct((hidden, rows, residues), NARROW),
        in_specs=[ANY] * len(deps) + [SMEM] * 2 + [VMEM] * (4 + len(pairs) + len(ready)),
        out_specs=VMEM,
        scratch_shapes=edge_scratch(fresh, hidden, residues),
        compiler_params=pltpu.CompilerParams(vmem_limit_bytes=16 << 20),
        cost_estimate=cost,
        name="edges",
    )(*deps, me, chain, mask, gain, gate, value, *pairs, *ready)


def left_call(deps, unit, base, span, offsets, cost, me, chain, mask, gain, gate, value, pairs):
    rows = sum(p.shape[0] for p in pairs)
    residues = pairs[0].shape[1]
    hidden = gate.shape[1]
    shapes = [jax.ShapeDtypeStruct((hidden * rows, LANES), WIDE_TYPE)] * (residues // LANES)
    return pl.pallas_call(
        behind(functools.partial(left_kernel, unit, base, span, offsets), len(deps)),
        out_shape=shapes,
        in_specs=[ANY] * len(deps) + [SMEM] * 2 + [VMEM] * (4 + len(pairs)),
        out_specs=[VMEM] * len(shapes),
        compiler_params=pltpu.CompilerParams(vmem_limit_bytes=16 << 20),
        cost_estimate=cost,
        name="left_edges",
    )(*deps, me, chain, mask, gain, gate, value, *pairs)


def triangle_call(deps, order, me, middle_gain, gain, output_gate, output_value, right, pairs, lefts):
    _, _, channels = pairs[0].shape
    rows = sum(p.shape[0] for p in pairs)
    hidden = output_value.shape[0]
    width = right[0].shape[1]
    tensors = [gain, output_gate, output_value, *right, *pairs]
    for left in lefts:
        tensors += left
    return pl.pallas_call(
        behind(functools.partial(triangle_kernel, len(pairs), order), len(deps)),
        out_shape=[jax.ShapeDtypeStruct((rows, width, channels), NARROW)] * len(order),
        in_specs=[ANY] * len(deps) + [SMEM] * 2 + [VMEM] * len(tensors),
        out_specs=[VMEM] * len(order),
        scratch_shapes=[pltpu.VMEM((hidden * rows, LANES), WIDE_TYPE)],
        compiler_params=pltpu.CompilerParams(vmem_limit_bytes=40 << 20),
        cost_estimate=pl.CostEstimate(flops=1 << 20, bytes_accessed=1 << 10, transcendentals=0),
        name="triangle",
    )(*deps, me, middle_gain, *tensors)


def place_call(places, base, rows, me, blocks, shape):
    return pl.pallas_call(
        functools.partial(place_kernel, places, base, rows),
        out_shape=jax.ShapeDtypeStruct(shape, NARROW),
        in_specs=[SMEM] + [ANY] * len(blocks),
        out_specs=ANY,
        scratch_shapes=[pltpu.SemaphoreType.DMA((sum(len(parts) for _, parts in places),))],
        compiler_params=pltpu.CompilerParams(vmem_limit_bytes=8 << 20),
        name="place",
    )(me, *blocks)


def hold_kernel(*refs):
    pass


def hold(value, *deps, cost=SHORT):
    return pl.pallas_call(
        hold_kernel,
        out_shape=jax.ShapeDtypeStruct(value.shape, value.dtype),
        in_specs=[ANY] * (1 + len(deps)),
        out_specs=ANY,
        input_output_aliases={0: 0},
        compiler_params=pltpu.CompilerParams(vmem_limit_bytes=1 << 20),
        cost_estimate=cost,
        name="hold",
    )(value, *deps)


def split_kernel(count, in_ref, *rest):
    out_refs, sem = rest[:count], rest[count]
    size = in_ref.shape[0] // count
    copies = [
        pltpu.make_async_copy(in_ref.at[pl.ds(n * size, size)], out_refs[n], sem.at[n]) for n in range(count)
    ]
    for copy in copies:
        copy.start()
    for copy in copies:
        copy.wait()


def split_call(values, count):
    shape = (values.shape[0] // count, *values.shape[1:])
    return pl.pallas_call(
        functools.partial(split_kernel, count),
        out_shape=[jax.ShapeDtypeStruct(shape, values.dtype)] * count,
        in_specs=[ANY],
        out_specs=[VMEM] * count,
        scratch_shapes=[pltpu.SemaphoreType.DMA((count,))],
        compiler_params=pltpu.CompilerParams(vmem_limit_bytes=8 << 20),
        cost_estimate=SHORT,
        name="split",
    )(values)


def make_shards(count):
    bits = [1 << b for b in range(count.bit_length() - 1)]
    near_bit, far_bit, low_bit = bits[0], bits[-1], bits[-2]
    side_bits = bits[1:-2][::-1]
    base = (far_bit, low_bit)

    def swap(values, mask):
        return lax.ppermute(values, "wide", [(d, d ^ mask) for d in range(count)])

    def cross(values):
        inner = lambda d: bool(d & far_bit) != bool(d & low_bit)
        pairs = [(d, d ^ far_bit ^ low_bit if inner(d) else d) for d in range(count)]
        return lax.ppermute(values, "wide", pairs)

    def shards(
        pair,
        residue_mask,
        input_gain,
        left_gate,
        left_value,
        right_gate,
        right_value,
        middle_gain,
        output_gate,
        output_value,
    ):
        rows = pair.shape[0]
        me = lax.axis_index("wide").astype(jnp.int32).reshape(1)
        mask = residue_mask.reshape(1, -1)
        gain = input_gain.reshape(1, -1)
        half = rows // 2
        offsets = (0, half)
        own = split_call(pair, 2)

        def right_edges(deps, unit, offset, raws, ready=(), cost=SHORT):
            return edge_call(
                deps, unit, offset, rows, cost, me, residue_mask, mask, gain, right_gate, right_value, raws, ready
            )

        def piece_edges(weights, shift, deps, unit, at, cost, raws):
            return left_call(
                deps, unit, shift, rows, at, cost, me, residue_mask, mask, gain, *weights, raws
            )

        right_piece = functools.partial(piece_edges, (right_gate, right_value), None)
        left_edges = functools.partial(piece_edges, (left_gate, left_value), base)

        blocks = []
        places = []

        def finish(deps, sources, lefts):
            pairs = [raw for _, _, raw in sources]
            outs = triangle_call(
                deps, order, me, middle_gain, gain, output_gate, output_value, rights, pairs, lefts
            )
            parts = [(unit, offset, raw.shape[0]) for unit, offset, raw in sources]
            for unit, out in zip(order, outs):
                blocks.append(out if unit == 0 else swap(out, unit))
                places.append((unit, parts))
            return outs[0]

        first = cross(pair)
        side = [swap(piece, low_bit) for piece in own]
        right = {0: right_edges((), 0, 0, own)}
        last = right[0]
        plain = {0: own[::-1]}
        for bit in side_bits:
            for unit in list(plain):
                plain[unit ^ bit] = [swap(piece, bit) for piece in plain[unit]]
        others = list(plain)[1:]
        side[0] = hold(side[0], last)
        side_ready = right_piece((last,), low_bit, (0,), SHORT, side[:1])
        last = side_ready[0]
        plain_ready = {}
        for unit in others:
            plain_ready[unit] = right_piece((last,), unit, (half,), SHORT, plain[unit][:1])
            last = plain_ready[unit][0]
        first = hold(first, last)
        left = left_edges((last,), 0, (0,), SHORT, [first])
        last = left[0]
        for unit in others:
            last = right[unit] = right_edges((last,), unit, 0, plain[unit][1:], plain_ready[unit])
        side[1] = hold(side[1], last)
        last = right[low_bit] = right_edges((last,), low_bit, half, side[1:], side_ready, LONG)
        both = {low_bit: side}
        for bit in side_bits:
            for unit in [unit ^ low_bit for unit in both]:
                across = hold(plain[unit ^ bit][0], plain_ready[unit ^ bit][0])
                there = [swap(both[unit ^ low_bit][0], bit), swap(across, low_bit)]
                both[unit ^ bit ^ low_bit] = there
        second = [cross(piece) for piece in side]
        first_near = swap(first, near_bit)
        left_near = left_edges((last,), near_bit, (0,), SHORT, [first_near])
        last = left_near[0]
        second[0] = hold(second[0], last)
        early = left_edges((), low_bit, (0,), SHORT, second[:1])
        last = early[0]
        for unit in list(both)[1:]:
            last = right[unit] = right_edges((last,), unit, 0, both[unit])
        order = [0] + list(right)[:0:-1]
        rights = [right[unit] for unit in order]
        early_near = swap(second[0], near_bit)
        left_early = left_edges((last,), low_bit ^ near_bit, (0,), SHORT, [early_near])
        done = finish(
            (),
            [(0, 0, first), (near_bit, 0, first_near), (low_bit, 0, second[0]), (low_bit ^ near_bit, 0, early_near)],
            [left, left_near, early, left_early],
        )

        late_raw = hold(second[1], done)
        late_near = swap(late_raw, near_bit)
        late = left_edges((done,), low_bit, (half,), SHORT, [late_raw])
        left_late = left_edges((late[0],), low_bit ^ near_bit, (half,), SHORT, [late_near])
        finish((), [(low_bit, half, late_raw), (low_bit ^ near_bit, half, late_near)], [late, left_late])
        return place_call(places, base, rows, me, blocks, (count * rows, rows, pair.shape[2]))

    return shards


def solution(mesh):
    in_specs = (P(("groups", "wide"), None, None), P("groups")) + (P(),) * 8
    out_specs = P("groups", "wide", None)
    return jax.shard_map(
        make_shards(mesh.shape["wide"]), mesh=mesh, in_specs=in_specs, out_specs=out_specs, check_vma=False
    )
```
